32 devices in a mesh: seq: 4 (over x, core), blk: 8 (over z, y).
Axes of the slice: x: 2, y: 2, z: 4, core: 2. Of those that a mesh axis runs over, the one named last changes fastest.
Arguments:
- tokens: bfloat16 [8192, 2048], P(('seq', 'blk')), may hold values from -6 to 6
- cotangent: bfloat16 [8192, 2048], P(('seq', 'blk')), may hold values from -6 to 6
- grouping: int32 [4, 1], P('seq'), may hold values from 0 to 1
- memory_start: float32 [4, 16, 128, 128], P('seq', 'blk'), may hold values from -128 to 128
- normalizer_start: float32 [4, 16, 128], P('seq', 'blk'), may hold values from 64 to 1024
- gain_attention: float32 [2048], replicated, may hold values from 0.1 to 1.9
- attention_in: bfloat16 [2048, 3, 2048], P('seq', None, 'blk'), may hold values from -0.125 to 0.125
- gate_logit: float32 [16], replicated, may hold values from -2.5 to 2.5
- attention_out: bfloat16 [2048, 2048], P('blk', 'seq'), may hold values from -0.5 to 0.5
- gain_feed: float32 [2048], replicated, may hold values from 0.1 to 1.9
- feed_in: bfloat16 [2048, 2, 8192], P('seq', None, 'blk'), may hold values from -0.125 to 0.125
- feed_out: bfloat16 [8192, 2048], P('blk', 'seq'), may hold values from -0.0625 to 0.0625
Outputs:
- mixed: bfloat16 [8192, 2048], P(('seq', 'blk'))
- token_grad: float32 [8192, 2048], P(('seq', 'blk'))
- gain_attention_grad: float32 [2048], replicated
- attention_in_grad: float32 [2048, 3, 2048], P('seq', None, 'blk')
- gate_logit_grad: float32 [16], replicated
- attention_out_grad: float32 [2048, 2048], P('blk', 'seq')
- gain_feed_grad: float32 [2048], replicated
- feed_in_grad: float32 [2048, 2, 8192], P('seq', None, 'blk')
- feed_out_grad: float32 [8192, 2048], P('blk', 'seq')
- memory_final: float32 [4, 16, 128, 128], P('seq', 'blk')
- normalizer_final: float32 [4, 16, 128], P('seq', 'blk')
The draws below stay inside these ranges and needn't reach their ends.
All inputs are finite; a program needn't handle non-finite values.
Results may differ from the reference program's by a relative error of at most 0.02.
Values may be sent and summed in bfloat16 or wider, within the bound.
No kernel may reach another device: no remote copies, remote signals or barrier semaphores. Data moves between devices by JAX's collectives and lax.ppermute only.
A program may use at most 320 MiB of HBM per device.

```python
import math
import jax
import jax.numpy as jnp
from jax import lax

D = 2048
HEADS = 16
HEAD = 128
FF = 8192
SHORT = 1024
SLOTS = 1
SEQS = 4
TOKENS = 8192


def with_ends(entries, own_key, least, top_value):
    longest = entries.shape.index(max(entries.shape))
    spots = []
    for shift in (0, 1):
        where = [jax.random.randint(jax.random.fold_in(own_key, axis), (), 0, length) for axis, length in enumerate(entries.shape)]
        where[longest] = (where[longest] + shift) % entries.shape[longest]
        spots.append(tuple(where))
    return entries.at[spots[0]].set(least).at[spots[1]].set(top_value)


def block_scale(rng, extent, split, least, largest):
    def one(position, blocks):
        heights = jax.random.uniform(jax.random.fold_in(jax.random.fold_in(rng, 6), position), (blocks,), jnp.float32, least / len(split), largest / len(split))
        return jnp.repeat(jnp.exp(heights), extent[position] // blocks).reshape((-1,) + (1,) * (len(extent) - position - 1))

    level = one(*split[0])
    for cut in split[1:]:
        level = level * one(*cut)
    return level


def normal_values(key, extent, spread, reach, pieces=(), held_as=jnp.bfloat16):
    array = jax.random.normal(key, extent, jnp.float32) * spread
    if len(pieces) > 0:
        array = block_scale(key, extent, pieces, -0.22, 0.18) * array
    return jnp.clip(array, min=-reach, max=reach).astype(held_as)


def setup_inputs(seed: int = 0) -> dict:
    arg_keys = jax.random.split(jax.random.key(seed), 13)
    tokens = normal_values(arg_keys[0], (TOKENS, D), 1.0, 6.0, ((0, 32),))
    cotangent = normal_values(arg_keys[1], (TOKENS, D), 1.0, 6.0, ((0, 32),))
    grouping = with_ends(jax.random.randint(arg_keys[2], (SEQS, SLOTS), 0, 2), jax.random.fold_in(arg_keys[2], 1), 0, 1).astype(jnp.int32)
    memory_start = normal_values(arg_keys[3], (SEQS, HEADS, HEAD, HEAD), 20.0, 128.0, ((0, 4), (1, 8)), jnp.float32)
    normalizer_start = jnp.clip(jnp.exp(math.log(1024.0) - 2.7725887 * jax.random.uniform(arg_keys[4], (SEQS, HEADS, HEAD), jnp.float32) ** block_scale(arg_keys[4], (SEQS, HEADS, HEAD), ((0, 4), (1, 8)), -0.2, 0.2)), 64.0, 1024.0)
    gain_attention = jnp.clip(1.0 + 0.18 * jax.random.normal(arg_keys[5], (D,), jnp.float32), 0.1, 1.9)
    attention_in = normal_values(arg_keys[6], (D, 3, D), D ** -0.5, 0.125, ((0, 4), (2, 8)))
    gate_logit = jnp.clip(jax.random.uniform(arg_keys[7], (HEADS,), jnp.float32, -2.5, 2.5), -2.5, 2.5)
    attention_out = normal_values(arg_keys[8], (D, D), (D // 16) ** -0.5, 0.5, ((0, 8), (1, 4)))
    gain_feed = jnp.clip(1.0 + 0.18 * jax.random.normal(arg_keys[9], (D,), jnp.float32), 0.1, 1.9)
    feed_in = normal_values(arg_keys[10], (D, 2, FF), D ** -0.5, 0.125, ((0, 4), (2, 8)))
    feed_out = normal_values(arg_keys[11], (FF, D), FF ** -0.5, 0.0625, ((0, 8), (1, 4)))
    return {"tokens": tokens, "cotangent": cotangent, "grouping": grouping, "memory_start": memory_start, "normalizer_start": normalizer_start, "gain_attention": gain_attention, "attention_in": attention_in, "gate_logit": gate_logit, "attention_out": attention_out, "gain_feed": gain_feed, "feed_in": feed_in, "feed_out": feed_out}


@jax.custom_vjp
def low(v):
    return lax.optimization_barrier(v.astype(jnp.bfloat16)).astype(jnp.float32)

@jax.custom_vjp
def low_back(v):
    return v

def low_keep(v):
    return (low(v), None)

def low_pass(kept, grad):
    return (grad,)

def back_keep(v):
    return (v, None)

def back_low(kept, grad):
    return (low(grad),)
low.defvjp(low_keep, low_pass)
low_back.defvjp(back_keep, back_low)
EPSILON = 1e-06
MASKED = -1e+30
PRECISE = lax.Precision.HIGHEST

def product(left, right):
    return jnp.dot(left, right, precision=PRECISE)

def normalize(values, gain):
    scale_rows = lax.rsqrt(lax.optimization_barrier(jnp.mean(values * values, axis=-1, keepdims=True)) + EPSILON)
    return low(values * scale_rows * gain)

def feature(values):
    return jax.nn.elu(values) + 1.0

def segment_table(splits, length):
    positions = jnp.arange(length, dtype=jnp.int32)
    slot = positions // (2 * SHORT)
    within = positions % (2 * SHORT)
    widths = 1 + splits
    before = jnp.cumsum(widths) - widths
    half = within // SHORT * splits[slot]
    segment = before[slot] + half
    begin = slot * (2 * SHORT) + half * SHORT
    return (segment.astype(jnp.int32), begin.astype(jnp.int32))

def project(tokens, gain_attention, attention_in):
    length = tokens.shape[0]
    joined = low(low_back(product(normalize(tokens, gain_attention), attention_in.reshape(D, 3 * D))))
    return tuple((joined[:, part * D:(part + 1) * D].reshape(length, HEADS, HEAD) for part in range(3)))

def memory_delta(key_feat, value_heads, member, memory, normalizer):
    numerator = jnp.einsum('tha,hab->thb', key_feat, memory, precision=PRECISE)
    denominator = jnp.einsum('tha,ha->th', key_feat, normalizer, precision=PRECISE)
    mismatch = value_heads - numerator / denominator[:, :, None]
    chosen = key_feat * member[:, None, None]
    return (jnp.einsum('tha,thb->hab', chosen, mismatch, precision=PRECISE), lax.optimization_barrier(jnp.sum(chosen, axis=0)))

def retrieve(query_feat, memory, normalizer):
    numerator = jnp.einsum('tha,hab->thb', query_feat, memory, precision=PRECISE)
    denominator = jnp.einsum('tha,ha->th', query_feat, normalizer, precision=PRECISE)
    return numerator / denominator[:, :, None]

def attention(query_heads, key_heads, value_heads, begin):
    length = query_heads.shape[0]
    block = min(512, length)
    count = length // block
    positions = jnp.arange(length, dtype=jnp.int32)

    def one_block(inputs):
        query_block, query_pos, query_begin = inputs
        scores = low_back(jnp.einsum('qhe,khe->hqk', query_block, key_heads, precision=PRECISE) * HEAD ** (-0.5))
        allowed = (positions[None, :] <= query_pos[:, None]) & (positions[None, :] >= query_begin[:, None])
        weights = low(jax.nn.softmax(jnp.where(allowed[None], scores, MASKED), axis=-1))
        return jnp.einsum('hqk,khe->qhe', weights, value_heads, precision=PRECISE)
    blocks = lax.map(jax.checkpoint(one_block), (query_heads.reshape(count, block, HEADS, HEAD), positions.reshape(count, block), begin.reshape(count, block)))
    return blocks.reshape(length, HEADS, HEAD)

def memory_chain(tokens, gain_attention, attention_in, segment, memory_zero, normalizer_zero, segments):
    query_heads, key_heads, value_heads = project(tokens, gain_attention, attention_in)
    key_feat = feature(key_heads)
    state_memory = [memory_zero]
    state_norm = [normalizer_zero]
    for part in range(segments):
        member = (segment == part).astype(jnp.float32)
        added, grown = memory_delta(key_feat, value_heads, member, state_memory[-1], state_norm[-1])
        state_memory.append(state_memory[-1] + added)
        state_norm.append(state_norm[-1] + grown)
    return (state_memory, state_norm)

def layer(tokens, gain_attention, attention_in, gate_logit, attention_out, gain_feed, feed_in, feed_out, segment, begin, state_memory, state_norm):
    length = tokens.shape[0]
    query_heads, key_heads, value_heads = project(tokens, gain_attention, attention_in)
    attended = low_back(attention(query_heads, key_heads, value_heads, begin))
    query_feat = feature(query_heads)
    key_feat = feature(key_heads)
    recalled = jnp.zeros_like(attended)
    for part in range(len(state_memory) - 1):
        if part == 0:
            memory, normalizer = (state_memory[0], state_norm[0])
        else:
            member = (segment == part - 1).astype(jnp.float32)
            added, grown = memory_delta(key_feat, value_heads, member, state_memory[part - 1], state_norm[part - 1])
            memory = state_memory[part - 1] + added
            normalizer = state_norm[part - 1] + grown
        recalled = jnp.where((segment == part)[:, None, None], retrieve(query_feat, memory, normalizer), recalled)
    mix = jax.nn.sigmoid(gate_logit)[None, :, None]
    merged = low((mix * recalled + (1.0 - mix) * attended).reshape(length, D))
    middle = tokens + low_back(product(merged, attention_out))
    normed_feed = normalize(middle, gain_feed)
    gate_up = low_back(product(normed_feed, feed_in.reshape(D, 2 * FF)))
    hidden = low(jax.nn.silu(gate_up[:, :FF]) * gate_up[:, FF:])
    return middle + low_back(product(hidden, feed_out))

def reference(tokens, cotangent, grouping, memory_start, normalizer_start, gain_attention, attention_in, gate_logit, attention_out, gain_feed, feed_in, feed_out):
    count = grouping.shape[0]
    segments = 2 * grouping.shape[1]
    length = tokens.shape[0] // count
    params = tuple((weight.astype(jnp.float32) for weight in (gain_attention, attention_in, gate_logit, attention_out, gain_feed, feed_in, feed_out)))

    def one_sequence(totals, inputs):
        rows, upstream, splits, memory_zero, normalizer_zero = inputs
        segment, begin = segment_table(splits, length)
        state_memory, state_norm = memory_chain(rows, params[0], params[1], segment, memory_zero, normalizer_zero, segments)

        def forward(rows, *weights):
            return layer(rows, *weights, segment, begin, state_memory, state_norm)
        result, pullback = jax.vjp(forward, rows, *params)
        grads = pullback(upstream)
        totals = tuple((total + grad for total, grad in zip(totals, grads[1:])))
        return (totals, (result, grads[0], state_memory[-1], state_norm[-1]))
    initial = tuple((jnp.zeros_like(weight) for weight in params))
    totals, outputs = lax.scan(one_sequence, initial, (tokens.astype(jnp.float32).reshape(count, length, D), cotangent.astype(jnp.float32).reshape(count, length, D), grouping, memory_start, normalizer_start))
    result, token_grad, memory_final, normalizer_final = outputs
    return (result.reshape(count * length, D).astype(jnp.bfloat16), token_grad.reshape(count * length, D), totals[0], totals[1], totals[2], totals[3], totals[4], totals[5], totals[6], memory_final, normalizer_final)
```

```python
import functools
import math

import jax
import jax.numpy as jnp
from jax import lax
from jax.experimental import pallas as pl
from jax.experimental.pallas import tpu as pltpu
from jax.sharding import PartitionSpec as P

SHORT = 1024
TILE = 512
EPSILON = 1e-06
MASKED = -1e30
LOG2E = math.log2(math.e)
VMEM_LIMIT = 48 * 1024 * 1024


def dot_nn(left, right):
    return lax.dot_general(left, right, (((1,), (0,)), ((), ())), preferred_element_type=jnp.float32)


def dot_nt(left, right):
    return lax.dot_general(left, right, (((1,), (1,)), ((), ())), preferred_element_type=jnp.float32)


def dot_tn(left, right):
    return lax.dot_general(left, right, (((0,), (0,)), ((), ())), preferred_element_type=jnp.float32)


def low(values):
    return values.astype(jnp.bfloat16)


def feature(values):
    return jnp.where(values > 0, values + 1.0, jnp.exp(jnp.minimum(values, 0.0)))


def first_key_tile(index, splits):
    per = 2 * SHORT // TILE
    slot = lax.div(index, per)
    second = (lax.rem(index, per) >= per // 2) & (splits[slot] == 1)
    return slot * per + jnp.where(second, per // 2, 0)


def tile_rows(index):
    return pl.ds(pl.multiple_of(index * TILE, TILE), TILE)


def causal(scores):
    key_pos = lax.broadcasted_iota(jnp.int32, scores.shape, 0)
    query_pos = lax.broadcasted_iota(jnp.int32, scores.shape, 1)
    return jnp.where(key_pos <= query_pos, scores, MASKED)


def state_matrix(memory, norm_row):
    spread = jnp.transpose(jnp.broadcast_to(norm_row, memory.shape))
    return low(jnp.concatenate([memory, spread], axis=1))


def forward_kernel(
    order, splits, mix, proj, memory, norm,
    merged, attended, lse, states, norms, memory_out, norm_out,
    q_s, k_s, v_s, vt_s, *, rows, heads, size,
):
    length = proj.shape[0]
    width = heads * size
    factor = size ** (-0.5) * LOG2E
    for b in range(length // rows):
        src = pl.ds(pl.multiple_of(order[b] * rows, rows), rows)
        dst = slice(b * rows, (b + 1) * rows)
        q_s[dst, :] = proj[src, 0:width]
        k_s[dst, :] = proj[src, width : 2 * width]
        value = proj[src, 2 * width : 3 * width]
        v_s[dst, :] = value
        vt_s[:, dst] = jnp.transpose(value)
    cols = [slice(h * size, (h + 1) * size) for h in range(heads)]

    def query_block(index, _):
        here = tile_rows(index)
        queries = [q_s[here, c] for c in cols]

        def scores_of(tile, h):
            return dot_nt(k_s[tile_rows(tile), cols[h]], queries[h]) * factor

        def weigh(tile, h, scores, highest):
            weights = jnp.exp2(scores - highest)
            total = jnp.sum(weights, axis=0, keepdims=True)
            return total, dot_nn(vt_s[cols[h], tile_rows(tile)], low(weights))

        start = []
        for h in range(heads):
            scores = causal(scores_of(index, h))
            highest = jnp.max(scores, axis=0, keepdims=True)
            start.append((highest, *weigh(index, h, scores, highest)))

        def step(tile, carry):
            out = []
            for h in range(heads):
                highest, total, acc = carry[h]
                scores = scores_of(tile, h)
                higher = jnp.maximum(highest, jnp.max(scores, axis=0, keepdims=True))
                keep = jnp.exp2(highest - higher)
                more, add = weigh(tile, h, scores, higher)
                out.append((higher, total * keep + more, acc * keep + add))
            return tuple(out)

        done = lax.fori_loop(first_key_tile(index, splits), index, step, tuple(start))
        for h in range(heads):
            highest, total, acc = done[h]
            attended[here, cols[h]] = jnp.transpose(acc / total)
            lse[index, h : h + 1, :] = highest + jnp.log2(total)
        return 0

    lax.fori_loop(0, length // TILE, query_block, 0)

    for h in range(heads):
        total_m, total_n = memory[h], norm[h : h + 1, :]
        now_m, now_n = total_m, total_n
        share = mix[h]
        for half in range(length // SHORT):
            fresh = True if half % 2 == 0 else splits[half // 2] == 1
            now_m = jnp.where(fresh, total_m, now_m)
            now_n = jnp.where(fresh, total_n, now_n)
            states[half, h] = now_m
            norms[half, h : h + 1, :] = now_n
            both = state_matrix(now_m, now_n)

            def chunk(index, carry):
                here = tile_rows(index)
                grown_m, grown_n = carry
                query_feat = feature(q_s[here, cols[h]].astype(jnp.float32))
                key_feat = feature(k_s[here, cols[h]].astype(jnp.float32))
                read = dot_nn(low(query_feat), both)
                recalled = read[:, :size] / read[:, size:]
                merged[here, cols[h]] = low(share * recalled + (1.0 - share) * attended[here, cols[h]])
                back = dot_nn(low(key_feat), both)
                miss = v_s[here, cols[h]].astype(jnp.float32) - back[:, :size] / back[:, size:]
                return (
                    grown_m + dot_tn(low(key_feat), low(miss)),
                    grown_n + jnp.sum(key_feat, axis=0, keepdims=True),
                )

            per = SHORT // TILE
            total_m, total_n = lax.fori_loop(half * per, (half + 1) * per, chunk, (total_m, total_n))
        memory_out[h] = total_m
        norm_out[h : h + 1, :] = total_n


def backward_kernel(
    order, splits, mix, proj, combined_grad, attended, lse, states, norms,
    proj_grad, gate,
    q_s, k_s, v_s, kt_s, g_s, delta_s, dq_s, dk_s, dv_s, *, rows, heads, size,
):
    length = proj.shape[0]
    width = heads * size
    scale = size ** (-0.5)
    factor = scale * LOG2E
    for b in range(length // rows):
        src = pl.ds(pl.multiple_of(order[b] * rows, rows), rows)
        dst = slice(b * rows, (b + 1) * rows)
        q_s[dst, :] = proj[src, 0:width]
        key = proj[src, width : 2 * width]
        k_s[dst, :] = key
        v_s[dst, :] = proj[src, 2 * width : 3 * width]
        kt_s[:, dst] = jnp.transpose(key)
    cols = [slice(h * size, (h + 1) * size) for h in range(heads)]
    ones = jnp.ones((8, size), jnp.float32)
    slots = length // (2 * SHORT)
    per = SHORT // TILE

    for h in range(heads):
        share = mix[h]
        col = cols[h]
        gate_sum = jnp.zeros((1, size), jnp.float32)
        next_m, next_n = jnp.zeros((size, size), jnp.float32), jnp.zeros((1, size), jnp.float32)
        for slot in reversed(range(slots)):
            split = splits[slot] == 1
            later_m, later_n = None, None
            for half in (2 * slot + 1, 2 * slot):
                last = half == 2 * slots - 1
                if half % 2 == 1:
                    up_m, up_n = next_m, next_n
                else:
                    up_m = jnp.where(split, later_m, next_m)
                    up_n = jnp.where(split, later_n, next_n)
                memory = states[half, h]
                norm_row = norms[half, h : h + 1, :]
                both = state_matrix(memory, norm_row)
                low_memory = low(memory)
                low_up = low(up_m)
                up_both = jnp.concatenate([low_up, low_memory], axis=1)

                def chunk(index, carry, both=both, low_memory=low_memory, low_up=low_up, up_both=up_both, norm_row=norm_row, up_n=up_n, last=last):
                    here = tile_rows(index)
                    sum_m, sum_n, sum_gate = carry
                    att = attended[here, col]
                    grad = combined_grad[here, col].astype(jnp.float32)
                    query_feat = feature(q_s[here, col].astype(jnp.float32))
                    read = dot_nn(low(query_feat), both)
                    inverse = 1.0 / read[:, size:]
                    recalled = read[:, :size] * inverse
                    recalled_grad = share * grad
                    attended_grad = low((1.0 - share) * grad)
                    g_s[here, col] = attended_grad
                    sums = lax.dot_general(
                        ones, attended_grad.astype(jnp.float32) * att, (((1,), (1,)), ((), ())),
                        precision=lax.Precision.HIGHEST, preferred_element_type=jnp.float32,
                    )
                    delta_s[index, h : h + 1, :] = sums[0:1, :]
                    sum_gate = sum_gate + jnp.sum(grad * (recalled - att), axis=0, keepdims=True)
                    scaled = recalled_grad * inverse
                    den_grad = -jnp.sum(recalled_grad * recalled, axis=1, keepdims=True) * inverse
                    query_feat_grad = dot_nt(low(scaled), low_memory) + den_grad * norm_row
                    dq_s[here, col] = query_feat_grad * jnp.minimum(query_feat, 1.0)
                    sum_m = sum_m + dot_tn(low(query_feat), low(scaled))
                    sum_n = sum_n + jnp.sum(den_grad * query_feat, axis=0, keepdims=True)
                    if last:
                        dk_s[here, col] = jnp.zeros((TILE, size), jnp.float32)
                        dv_s[here, col] = jnp.zeros((TILE, size), jnp.float32)
                    else:
                        key_feat = feature(k_s[here, col].astype(jnp.float32))
                        back = dot_nn(low(key_feat), both)
                        key_inverse = 1.0 / back[:, size:]
                        retrieved = back[:, :size] * key_inverse
                        miss = v_s[here, col].astype(jnp.float32) - retrieved
                        miss_grad = dot_nn(low(key_feat), low_up)
                        dv_s[here, col] = miss_grad
                        pair = jnp.concatenate([low(miss), low(-miss_grad * key_inverse)], axis=1)
                        along = jnp.sum(miss_grad * retrieved, axis=1, keepdims=True) * key_inverse
                        key_feat_grad = dot_nt(pair, up_both) + along * norm_row + up_n
                        dk_s[here, col] = key_feat_grad * jnp.minimum(key_feat, 1.0)
                    return sum_m, sum_n, sum_gate

                sum_m, sum_n, gate_sum = lax.fori_loop(
                    half * per, (half + 1) * per, chunk,
                    (jnp.zeros((size, size), jnp.float32), jnp.zeros((1, size), jnp.float32), gate_sum),
                )
                if half % 2 == 1:
                    later_m, later_n = sum_m, sum_n
                else:
                    next_m = jnp.where(split, sum_m, sum_m + later_m)
                    next_n = jnp.where(split, sum_n, sum_n + later_n)
        gate[h : h + 1, :] = gate_sum

    def query_block(index, _):
        here = tile_rows(index)

        def part(tile, h, mask):
            there = tile_rows(tile)
            col = cols[h]
            queries, grads, keys = q_s[here, col], g_s[here, col], k_s[there, col]
            scores = dot_nt(keys, queries) * factor
            if mask:
                scores = causal(scores)
            probs = jnp.exp2(scores - lse[index, h : h + 1, :])
            prob_grad = dot_nt(v_s[there, col], grads)
            score_grad = low(probs * (prob_grad - delta_s[index, h : h + 1, :]))
            dv_s[there, col] += dot_nn(low(probs), grads)
            dk_s[there, col] += dot_nn(score_grad, queries) * scale
            return dot_nn(kt_s[col, there], score_grad)

        start = tuple(part(index, h, True) for h in range(heads))

        def step(tile, carry):
            return tuple(carry[h] + part(tile, h, False) for h in range(heads))

        done = lax.fori_loop(first_key_tile(index, splits), index, step, start)
        for h in range(heads):
            dq_s[here, cols[h]] += jnp.transpose(done[h]) * scale
        return 0

    lax.fori_loop(0, length // TILE, query_block, 0)
    for b in range(length // rows):
        dst = pl.ds(pl.multiple_of(order[b] * rows, rows), rows)
        src = slice(b * rows, (b + 1) * rows)
        proj_grad[dst, 0:width] = low(dq_s[src, :])
        proj_grad[dst, width : 2 * width] = low(dk_s[src, :])
        proj_grad[dst, 2 * width : 3 * width] = low(dv_s[src, :])


SMEM = pl.BlockSpec(memory_space=pltpu.SMEM)
VMEM = pl.BlockSpec(memory_space=pltpu.VMEM)


def attend_forward(order, splits, mix, proj, memory, norm, rows):
    heads, size, _ = memory.shape
    length, width = proj.shape[0], heads * size
    halves, tiles = length // SHORT, length // TILE
    shapes = [
        jax.ShapeDtypeStruct((length, width), jnp.bfloat16),
        jax.ShapeDtypeStruct((length, width), jnp.float32),
        jax.ShapeDtypeStruct((tiles, heads, TILE), jnp.float32),
        jax.ShapeDtypeStruct((halves, heads, size, size), jnp.float32),
        jax.ShapeDtypeStruct((halves, heads, size), jnp.float32),
        jax.ShapeDtypeStruct((heads, size, size), jnp.float32),
        jax.ShapeDtypeStruct((heads, size), jnp.float32),
    ]
    whole = pltpu.VMEM((length, width), jnp.bfloat16)
    return pl.pallas_call(
        functools.partial(forward_kernel, rows=rows, heads=heads, size=size),
        out_shape=shapes,
        in_specs=[SMEM] * 3 + [VMEM] * 3,
        out_specs=[VMEM] * len(shapes),
        scratch_shapes=[whole, whole, whole, pltpu.VMEM((width, length), jnp.bfloat16)],
        compiler_params=pltpu.CompilerParams(vmem_limit_bytes=VMEM_LIMIT),
        cost_estimate=pl.CostEstimate(
            flops=4 * length * length * width, bytes_accessed=12 * length * width, transcendentals=0
        ),
    )(order, splits, mix, proj, memory, norm)


def attend_backward(order, splits, mix, proj, combined_grad, attended, lse, states, norms, rows):
    _, heads, size, _ = states.shape
    length, width = proj.shape[0], heads * size
    tiles = length // TILE
    shapes = [
        jax.ShapeDtypeStruct((length, 3 * width), jnp.bfloat16),
        jax.ShapeDtypeStruct((heads, size), jnp.float32),
    ]
    whole = pltpu.VMEM((length, width), jnp.bfloat16)
    wide = pltpu.VMEM((length, width), jnp.float32)
    return pl.pallas_call(
        functools.partial(backward_kernel, rows=rows, heads=heads, size=size),
        out_shape=shapes,
        in_specs=[SMEM] * 3 + [VMEM] * 6,
        out_specs=[VMEM] * len(shapes),
        scratch_shapes=[
            whole, whole, whole, pltpu.VMEM((width, length), jnp.bfloat16), whole,
            pltpu.VMEM((tiles, heads, TILE), jnp.float32), wide, wide, wide,
        ],
        compiler_params=pltpu.CompilerParams(vmem_limit_bytes=VMEM_LIMIT),
        cost_estimate=pl.CostEstimate(
            flops=10 * length * length * width, bytes_accessed=20 * length * width, transcendentals=0
        ),
    )(order, splits, mix, proj, combined_grad, attended, lse, states, norms)


def ring_of(count):
    deep = 4 if count % 4 == 0 else count
    across = count // deep
    ring = [z * across for z in range(deep)]
    for z in reversed(range(deep)):
        turn = range(1, across)
        ring += [z * across + y for y in (turn if (deep - 1 - z) % 2 == 0 else reversed(turn))]
    return ring


class Ring:
    def __init__(self, count):
        self.count = count
        ring = ring_of(count)
        self.ahead = [(ring[p], ring[(p + 1) % count]) for p in range(count)]
        self.behind = [(b, a) for a, b in self.ahead]
        places = [0] * count
        for place, index in enumerate(ring):
            places[index] = place
        places = jnp.array(places, jnp.int32)
        self.order = lax.rem(places - places[lax.axis_index("blk")] + count, count)

    def forth(self, values):
        return lax.ppermute(values, "blk", self.ahead)

    def back(self, values):
        return lax.ppermute(values, "blk", self.behind)

    def gather(self, block):
        half = self.count // 2
        middle = block.shape[0] // 2
        blocks = {0: block}
        arrival = [0]
        from_behind = from_ahead = block
        for step in range(1, half):
            from_behind = self.forth(from_behind)
            from_ahead = self.back(from_ahead)
            blocks[self.count - step] = from_behind
            blocks[step] = from_ahead
            arrival += [self.count - step, step]
        blocks[half] = jnp.concatenate([self.forth(from_behind[:middle]), self.back(from_ahead[middle:])])
        arrival.append(half)
        return blocks, arrival

    def scatter(self, partial):
        half = self.count // 2
        far = low(partial(half))
        middle = far.shape[0] // 2
        forward = self.forth(far[:middle])
        backward = self.back(far[middle:])
        for step in range(half - 1, 0, -1):
            forward, backward = forward.astype(jnp.float32), backward.astype(jnp.float32)
            if step == half - 1:
                forward = jnp.pad(forward, ((0, middle), (0, 0)))
                backward = jnp.pad(backward, ((middle, 0), (0, 0)))
            forward = self.forth(low(partial(step) + forward))
            backward = self.back(low(partial(self.count - step) + backward))
        return partial(0) + forward.astype(jnp.float32) + backward.astype(jnp.float32)


def sum_everywhere(values):
    for axis in ("seq", "blk"):
        size = lax.axis_size(axis)
        step = 1
        while step < size:
            values = values + lax.ppermute(values, axis, [(i, i ^ step) for i in range(size)])
            step *= 2
    return values


def rms_parts(values):
    scale_rows = lax.rsqrt(jnp.mean(values * values, axis=-1, keepdims=True) + EPSILON)
    return (scale_rows, values * scale_rows)


def rms_back(unit_grad, unit, scale_rows):
    return scale_rows * (unit_grad - unit * jnp.mean(unit_grad * unit, axis=-1, keepdims=True))


def joined(blocks):
    return jnp.concatenate([blocks[d] for d in range(len(blocks))])


def sum_over_seq(values, dimension):
    return lax.psum_scatter(low(values), "seq", scatter_dimension=dimension, tiled=True)


def per_device(
    tokens,
    cotangent,
    grouping,
    memory_start,
    normalizer_start,
    gain_attention,
    attention_in,
    gate_logit,
    attention_out,
    gain_feed,
    feed_in,
    feed_out,
):
    rows, width = tokens.shape
    heads_here = memory_start.shape[1]
    count = lax.axis_size("blk")
    ring = Ring(count)
    splits = grouping[0]
    head_first = lax.axis_index("blk") * heads_here
    mix = jax.nn.sigmoid(lax.dynamic_slice_in_dim(gate_logit, head_first, heads_here, 0))

    def whole(weight, axis):
        return lax.all_gather(weight, "seq", axis=axis, tiled=True)

    w_in = whole(attention_in.reshape(attention_in.shape[0], -1), 0)
    w_out = whole(lax.all_gather(attention_out, "blk", axis=0, tiled=True), 1)
    f_in = whole(feed_in.reshape(feed_in.shape[0], -1), 0)
    f_out = whole(feed_out, 1)
    hidden_here = f_out.shape[0]

    tokens_full = tokens.astype(jnp.float32)
    scale_first, unit_first = rms_parts(tokens_full)
    normed_a, arrival = ring.gather(low(unit_first * gain_attention))
    proj = joined({d: low(dot_nn(normed_a[d], w_in)) for d in arrival})
    merged, attended, lse, states, norms, memory_final, norm_final = attend_forward(
        ring.order, splits, mix, proj, memory_start[0], normalizer_start[0], rows
    )
    merged_mine = lax.all_to_all(merged, "blk", 0, 1, tiled=True)
    middle = tokens_full + dot_nn(merged_mine, w_out)
    scale_second, unit_second = rms_parts(middle)

    cot, _ = ring.gather(cotangent)
    normed_f, arrival = ring.gather(low(unit_second * gain_feed))
    hidden, gate_up_grad = {}, {}
    for d in arrival:
        gate_up = dot_nn(normed_f[d], f_in)
        gate, up = gate_up[:, :hidden_here], gate_up[:, hidden_here:]
        sigmoid_gate = jax.nn.sigmoid(gate)
        activated = gate * sigmoid_gate
        hidden[d] = low(activated * up)
        hidden_grad = dot_nt(cot[d], f_out)
        gate_grad = hidden_grad * up * sigmoid_gate * (1.0 + gate * (1.0 - sigmoid_gate))
        gate_up_grad[d] = low(jnp.concatenate([gate_grad, hidden_grad * activated], axis=1))
    normed_f_grad = ring.scatter(lambda d: dot_nt(gate_up_grad[d], f_in))
    gain_feed_part = jnp.sum(normed_f_grad * unit_second, axis=0)
    middle_grad = cotangent.astype(jnp.float32) + rms_back(
        normed_f_grad * gain_feed, unit_second, scale_second
    )
    out_grad = low(middle_grad)
    combined_grad = lax.all_to_all(low(dot_nt(out_grad, w_out)), "blk", 1, 0, tiled=True)
    proj_grad, gate_rows = attend_backward(
        ring.order, splits, mix, proj, combined_grad, attended, lse, states, norms, rows
    )
    result = middle + ring.scatter(lambda d: dot_nn(hidden[d], f_out))

    normed_a_grad = ring.scatter(lambda d: dot_nt(proj_grad[d * rows : (d + 1) * rows], w_in))
    token_grad = middle_grad + rms_back(normed_a_grad * gain_attention, unit_first, scale_first)

    feed_out_grad = sum_over_seq(dot_tn(joined(hidden), joined(cot)), 1)
    feed_in_grad = sum_over_seq(dot_tn(joined(normed_f), joined(gate_up_grad)), 0)
    attention_out_grad = lax.psum_scatter(
        sum_over_seq(dot_tn(merged_mine, out_grad), 1), "blk", scatter_dimension=0, tiled=True
    )
    attention_in_local = dot_tn(joined(normed_a), proj_grad)
    attention_in_grad = sum_over_seq(attention_in_local, 0)
    gain_attention_part = jnp.sum(attention_in_local * w_in.astype(jnp.float32), axis=1) / gain_attention
    gate_part = jnp.sum(gate_rows, axis=1) * mix * (1.0 - mix)
    gate_full = lax.dynamic_update_slice_in_dim(
        jnp.zeros(gate_logit.shape, jnp.float32), gate_part, head_first, 0
    )
    sums = sum_everywhere(jnp.concatenate([gain_attention_part, gain_feed_part, gate_full]))
    return (
        low(result),
        token_grad,
        sums[:width],
        attention_in_grad.astype(jnp.float32).reshape(attention_in.shape),
        sums[2 * width :],
        attention_out_grad.astype(jnp.float32),
        sums[width : 2 * width],
        feed_in_grad.astype(jnp.float32).reshape(feed_in.shape),
        feed_out_grad.astype(jnp.float32),
        memory_final[None],
        norm_final[None],
    )


def solution(mesh):
    in_specs = (
        P(("seq", "blk"), None),
        P(("seq", "blk"), None),
        P("seq", None),
        P("seq", "blk", None, None),
        P("seq", "blk", None),
        P(),
        P("seq", None, "blk"),
        P(),
        P("blk", "seq"),
        P(),
        P("seq", None, "blk"),
        P("blk", "seq"),
    )
    out_specs = (
        P(("seq", "blk"), None),
        P(("seq", "blk"), None),
        P(),
        P("seq", None, "blk"),
        P(),
        P("blk", "seq"),
        P(),
        P("seq", None, "blk"),
        P("blk", "seq"),
        P("seq", "blk", None, None),
        P("seq", "blk", None),
    )
    return jax.shard_map(
        per_device, mesh=mesh, in_specs=in_specs, out_specs=out_specs, check_vma=False
    )
```

```python
import functools
import math

import jax
import jax.numpy as jnp
from jax import lax
from jax.experimental import pallas as pl
from jax.experimental.pallas import tpu as pltpu
from jax.sharding import PartitionSpec as P

SHORT = 1024
TILE = 512
FEED_TILE = 256
EPSILON = 1e-06
MASKED = -1e30
LOG2E = math.log2(math.e)
VMEM_LIMIT = 60 * 1024 * 1024


def dot_nn(left, right):
    return lax.dot_general(left, right, (((1,), (0,)), ((), ())), preferred_element_type=jnp.float32)


def dot_nt(left, right):
    return lax.dot_general(left, right, (((1,), (1,)), ((), ())), preferred_element_type=jnp.float32)


def dot_tn(left, right):
    return lax.dot_general(left, right, (((0,), (0,)), ((), ())), preferred_element_type=jnp.float32)


def low(values):
    return values.astype(jnp.bfloat16)


def feature(values):
    return jnp.where(values > 0, values + 1.0, jnp.exp(jnp.minimum(values, 0.0)))


def first_key_tile(index, splits):
    per = 2 * SHORT // TILE
    slot = lax.div(index, per)
    second = (lax.rem(index, per) >= per // 2) & (splits[slot] == 1)
    return slot * per + jnp.where(second, per // 2, 0)


def tile_rows(index):
    return pl.ds(pl.multiple_of(index * TILE, TILE), TILE)


def causal(scores):
    key_pos = lax.broadcasted_iota(jnp.int32, scores.shape, 0)
    query_pos = lax.broadcasted_iota(jnp.int32, scores.shape, 1)
    return jnp.where(key_pos <= query_pos, scores, MASKED)


def state_matrix(memory, norm_row):
    spread = jnp.transpose(jnp.broadcast_to(norm_row, memory.shape))
    return low(jnp.concatenate([memory, spread], axis=1))


def forward_kernel(
    order, splits, mix, proj, memory, norm,
    merged, attended, lse, states, norms, memory_out, norm_out,
    q_s, k_s, v_s, vt_s, *, rows, heads, size,
):
    length = proj.shape[0]
    width = heads * size
    factor = size ** (-0.5) * LOG2E
    for b in range(length // rows):
        src = pl.ds(pl.multiple_of(order[b] * rows, rows), rows)
        dst = slice(b * rows, (b + 1) * rows)
        q_s[dst, :] = proj[src, 0:width]
        k_s[dst, :] = proj[src, width : 2 * width]
        value = proj[src, 2 * width : 3 * width]
        v_s[dst, :] = value
        vt_s[:, dst] = jnp.transpose(value)
    cols = [slice(h * size, (h + 1) * size) for h in range(heads)]

    def query_block(index, _):
        here = tile_rows(index)
        queries = [q_s[here, c] for c in cols]

        def scores_of(tile, h):
            return dot_nt(k_s[tile_rows(tile), cols[h]], queries[h]) * factor

        def weigh(tile, h, scores, highest):
            weights = jnp.exp2(scores - highest)
            total = jnp.sum(weights, axis=0, keepdims=True)
            return total, dot_nn(vt_s[cols[h], tile_rows(tile)], low(weights))

        start = []
        for h in range(heads):
            scores = causal(scores_of(index, h))
            highest = jnp.max(scores, axis=0, keepdims=True)
            start.append((highest, *weigh(index, h, scores, highest)))

        def step(tile, carry):
            out = []
            for h in range(heads):
                highest, total, acc = carry[h]
                scores = scores_of(tile, h)
                higher = jnp.maximum(highest, jnp.max(scores, axis=0, keepdims=True))
                keep = jnp.exp2(highest - higher)
                more, add = weigh(tile, h, scores, higher)
                out.append((higher, total * keep + more, acc * keep + add))
            return tuple(out)

        done = lax.fori_loop(first_key_tile(index, splits), index, step, tuple(start))
        for h in range(heads):
            highest, total, acc = done[h]
            attended[here, cols[h]] = jnp.transpose(acc / total)
            lse[index, h : h + 1, :] = highest + jnp.log2(total)
        return 0

    lax.fori_loop(0, length // TILE, query_block, 0)

    for h in range(heads):
        total_m, total_n = memory[h], norm[h : h + 1, :]
        now_m, now_n = total_m, total_n
        share = mix[h]
        for half in range(length // SHORT):
            fresh = True if half % 2 == 0 else splits[half // 2] == 1
            now_m = jnp.where(fresh, total_m, now_m)
            now_n = jnp.where(fresh, total_n, now_n)
            states[half, h] = now_m
            norms[half, h : h + 1, :] = now_n
            both = state_matrix(now_m, now_n)

            def chunk(index, carry):
                here = tile_rows(index)
                grown_m, grown_n = carry
                query_feat = feature(q_s[here, cols[h]].astype(jnp.float32))
                key_feat = feature(k_s[here, cols[h]].astype(jnp.float32))
                read = dot_nn(low(query_feat), both)
                recalled = read[:, :size] / read[:, size:]
                merged[here, cols[h]] = low(share * recalled + (1.0 - share) * attended[here, cols[h]])
                back = dot_nn(low(key_feat), both)
                miss = v_s[here, cols[h]].astype(jnp.float32) - back[:, :size] / back[:, size:]
                return (
                    grown_m + dot_tn(low(key_feat), low(miss)),
                    grown_n + jnp.sum(key_feat, axis=0, keepdims=True),
                )

            per = SHORT // TILE
            total_m, total_n = lax.fori_loop(half * per, (half + 1) * per, chunk, (total_m, total_n))
        memory_out[h] = total_m
        norm_out[h : h + 1, :] = total_n


def backward_kernel(
    order, splits, mix, proj, combined_grad, attended, lse, states, norms,
    proj_grad, gate,
    q_s, k_s, v_s, kt_s, g_s, delta_s, dq_s, dk_s, dv_s, *, rows, heads, size,
):
    length = proj.shape[0]
    width = heads * size
    scale = size ** (-0.5)
    factor = scale * LOG2E
    for b in range(length // rows):
        src = pl.ds(pl.multiple_of(order[b] * rows, rows), rows)
        dst = slice(b * rows, (b + 1) * rows)
        q_s[dst, :] = proj[src, 0:width]
        key = proj[src, width : 2 * width]
        k_s[dst, :] = key
        v_s[dst, :] = proj[src, 2 * width : 3 * width]
        kt_s[:, dst] = jnp.transpose(key)
    cols = [slice(h * size, (h + 1) * size) for h in range(heads)]
    ones = jnp.ones((8, size), jnp.float32)
    slots = length // (2 * SHORT)
    per = SHORT // TILE

    for h in range(heads):
        share = mix[h]
        col = cols[h]
        gate_sum = jnp.zeros((1, size), jnp.float32)
        next_m, next_n = jnp.zeros((size, size), jnp.float32), jnp.zeros((1, size), jnp.float32)
        for slot in reversed(range(slots)):
            split = splits[slot] == 1
            later_m, later_n = None, None
            for half in (2 * slot + 1, 2 * slot):
                last = half == 2 * slots - 1
                if half % 2 == 1:
                    up_m, up_n = next_m, next_n
                else:
                    up_m = jnp.where(split, later_m, next_m)
                    up_n = jnp.where(split, later_n, next_n)
                memory = states[half, h]
                norm_row = norms[half, h : h + 1, :]
                both = state_matrix(memory, norm_row)
                low_memory = low(memory)
                low_up = low(up_m)
                up_both = jnp.concatenate([low_up, low_memory], axis=1)

                def chunk(index, carry, both=both, low_memory=low_memory, low_up=low_up, up_both=up_both, norm_row=norm_row, up_n=up_n, last=last):
                    here = tile_rows(index)
                    sum_m, sum_n, sum_gate = carry
                    att = attended[here, col]
                    grad = combined_grad[here, col].astype(jnp.float32)
                    query_feat = feature(q_s[here, col].astype(jnp.float32))
                    read = dot_nn(low(query_feat), both)
                    inverse = 1.0 / read[:, size:]
                    recalled = read[:, :size] * inverse
                    recalled_grad = share * grad
                    attended_grad = low((1.0 - share) * grad)
                    g_s[here, col] = attended_grad
                    sums = lax.dot_general(
                        ones, attended_grad.astype(jnp.float32) * att, (((1,), (1,)), ((), ())),
                        precision=lax.Precision.HIGHEST, preferred_element_type=jnp.float32,
                    )
                    delta_s[index, h : h + 1, :] = sums[0:1, :]
                    sum_gate = sum_gate + jnp.sum(grad * (recalled - att), axis=0, keepdims=True)
                    scaled = recalled_grad * inverse
                    den_grad = -jnp.sum(recalled_grad * recalled, axis=1, keepdims=True) * inverse
                    query_feat_grad = dot_nt(low(scaled), low_memory) + den_grad * norm_row
                    dq_s[here, col] = query_feat_grad * jnp.minimum(query_feat, 1.0)
                    sum_m = sum_m + dot_tn(low(query_feat), low(scaled))
                    sum_n = sum_n + jnp.sum(den_grad * query_feat, axis=0, keepdims=True)
                    if last:
                        dk_s[here, col] = jnp.zeros((TILE, size), jnp.float32)
                        dv_s[here, col] = jnp.zeros((TILE, size), jnp.float32)
                    else:
                        key_feat = feature(k_s[here, col].astype(jnp.float32))
                        back = dot_nn(low(key_feat), both)
                        key_inverse = 1.0 / back[:, size:]
                        retrieved = back[:, :size] * key_inverse
                        miss = v_s[here, col].astype(jnp.float32) - retrieved
                        miss_grad = dot_nn(low(key_feat), low_up)
                        dv_s[here, col] = miss_grad
                        pair = jnp.concatenate([low(miss), low(-miss_grad * key_inverse)], axis=1)
                        along = jnp.sum(miss_grad * retrieved, axis=1, keepdims=True) * key_inverse
                        key_feat_grad = dot_nt(pair, up_both) + along * norm_row + up_n
                        dk_s[here, col] = key_feat_grad * jnp.minimum(key_feat, 1.0)
                    return sum_m, sum_n, sum_gate

                sum_m, sum_n, gate_sum = lax.fori_loop(
                    half * per, (half + 1) * per, chunk,
                    (jnp.zeros((size, size), jnp.float32), jnp.zeros((1, size), jnp.float32), gate_sum),
                )
                if half % 2 == 1:
                    later_m, later_n = sum_m, sum_n
                else:
                    next_m = jnp.where(split, sum_m, sum_m + later_m)
                    next_n = jnp.where(split, sum_n, sum_n + later_n)
        gate[h : h + 1, :] = gate_sum

    def query_block(index, _):
        here = tile_rows(index)

        def part(tile, h, mask):
            there = tile_rows(tile)
            col = cols[h]
            queries, grads, keys = q_s[here, col], g_s[here, col], k_s[there, col]
            scores = dot_nt(keys, queries) * factor
            if mask:
                scores = causal(scores)
            probs = jnp.exp2(scores - lse[index, h : h + 1, :])
            prob_grad = dot_nt(v_s[there, col], grads)
            score_grad = low(probs * (prob_grad - delta_s[index, h : h + 1, :]))
            dv_s[there, col] += dot_nn(low(probs), grads)
            dk_s[there, col] += dot_nn(score_grad, queries) * scale
            return dot_nn(kt_s[col, there], score_grad)

        start = tuple(part(index, h, True) for h in range(heads))

        def step(tile, carry):
            return tuple(carry[h] + part(tile, h, False) for h in range(heads))

        done = lax.fori_loop(first_key_tile(index, splits), index, step, start)
        for h in range(heads):
            dq_s[here, cols[h]] += jnp.transpose(done[h]) * scale
        return 0

    lax.fori_loop(0, length // TILE, query_block, 0)
    for b in range(length // rows):
        dst = pl.ds(pl.multiple_of(order[b] * rows, rows), rows)
        src = slice(b * rows, (b + 1) * rows)
        proj_grad[dst, 0:width] = low(dq_s[src, :])
        proj_grad[dst, width : 2 * width] = low(dk_s[src, :])
        proj_grad[dst, 2 * width : 3 * width] = low(dv_s[src, :])


SMEM = pl.BlockSpec(memory_space=pltpu.SMEM)
VMEM = pl.BlockSpec(memory_space=pltpu.VMEM)


def attend_forward(order, splits, mix, proj, memory, norm, rows):
    heads, size, _ = memory.shape
    length, width = proj.shape[0], heads * size
    halves, tiles = length // SHORT, length // TILE
    shapes = [
        jax.ShapeDtypeStruct((length, width), jnp.bfloat16),
        jax.ShapeDtypeStruct((length, width), jnp.float32),
        jax.ShapeDtypeStruct((tiles, heads, TILE), jnp.float32),
        jax.ShapeDtypeStruct((halves, heads, size, size), jnp.float32),
        jax.ShapeDtypeStruct((halves, heads, size), jnp.float32),
        jax.ShapeDtypeStruct((heads, size, size), jnp.float32),
        jax.ShapeDtypeStruct((heads, size), jnp.float32),
    ]
    whole = pltpu.VMEM((length, width), jnp.bfloat16)
    return pl.pallas_call(
        functools.partial(forward_kernel, rows=rows, heads=heads, size=size),
        out_shape=shapes,
        in_specs=[SMEM] * 3 + [VMEM] * 3,
        out_specs=[VMEM] * len(shapes),
        scratch_shapes=[whole, whole, whole, pltpu.VMEM((width, length), jnp.bfloat16)],
        compiler_params=pltpu.CompilerParams(vmem_limit_bytes=VMEM_LIMIT),
        cost_estimate=NO_COST,
    )(order, splits, mix, proj, memory, norm)


def attend_backward(order, splits, mix, proj, combined_grad, attended, lse, states, norms, rows):
    _, heads, size, _ = states.shape
    length, width = proj.shape[0], heads * size
    tiles = length // TILE
    shapes = [
        jax.ShapeDtypeStruct((length, 3 * width), jnp.bfloat16),
        jax.ShapeDtypeStruct((heads, size), jnp.float32),
    ]
    whole = pltpu.VMEM((length, width), jnp.bfloat16)
    wide = pltpu.VMEM((length, width), jnp.float32)
    return pl.pallas_call(
        functools.partial(backward_kernel, rows=rows, heads=heads, size=size),
        out_shape=shapes,
        in_specs=[SMEM] * 3 + [VMEM] * 6,
        out_specs=[VMEM] * len(shapes),
        scratch_shapes=[
            whole, whole, whole, pltpu.VMEM((width, length), jnp.bfloat16), whole,
            pltpu.VMEM((tiles, heads, TILE), jnp.float32), wide, wide, wide,
        ],
        compiler_params=pltpu.CompilerParams(vmem_limit_bytes=VMEM_LIMIT),
        cost_estimate=NO_COST,
    )(order, splits, mix, proj, combined_grad, attended, lse, states, norms)


def fill(whole, pieces):
    rows = pieces[0].shape[0]
    for place, piece in enumerate(pieces):
        whole[place * rows : (place + 1) * rows, :] = piece[...]


def project_kernel(*refs, count):
    pieces, weight = refs[:count], refs[count]
    normed_all, proj_all = refs[-2:]
    rows, width = pieces[0].shape[0], normed_all.shape[1]

    @pl.when(pl.program_id(0) == 0)
    def _():
        for place, piece in enumerate(pieces):
            normed_all[place * rows : (place + 1) * rows, :] = piece[:, :width]

    proj_all[...] = low(dot_nn(normed_all[...], weight[...]))


def feed_kernel(*refs, count):
    normed, cots = refs[:count], refs[count : 2 * count]
    w_gate, w_up, w_down = refs[2 * count : 2 * count + 3]
    result_s, grad_s = refs[-2:]
    results, grads = refs[-2 - 2 * count : -2 - count], refs[-2 - count : -2]
    normed_all, cot_all, hidden, gate_grad, up_grad = refs[-7 - 2 * count : -2 - 2 * count]
    step = pl.program_id(0)

    @pl.when(step == 0)
    def _():
        fill(normed_all, normed)
        fill(cot_all, cots)

    gate = dot_nn(normed_all[...], w_gate[...])
    up = dot_nn(normed_all[...], w_up[...])
    hidden_grad = dot_nt(cot_all[...], w_down[...])
    sigmoid_gate = 1.0 / (1.0 + jnp.exp(-gate))
    activated = gate * sigmoid_gate
    low_hidden = low(activated * up)
    low_gate = low(hidden_grad * up * (sigmoid_gate + activated * (1.0 - sigmoid_gate)))
    low_up = low(hidden_grad * activated)
    hidden[...] = low_hidden
    gate_grad[...] = low_gate
    up_grad[...] = low_up
    more_result = dot_nn(low_hidden, w_down[...])
    more_grad = dot_nt(low_gate, w_gate[...]) + dot_nt(low_up, w_up[...])

    @pl.when(step == 0)
    def _():
        result_s[...] = more_result
        grad_s[...] = more_grad

    @pl.when(step > 0)
    def _():
        result_s[...] += more_result
        grad_s[...] += more_grad

    @pl.when(step == pl.num_programs(0) - 1)
    def _():
        rows = results[0].shape[0]
        for place in range(count):
            here = slice(place * rows, (place + 1) * rows)
            results[place][...] = low(result_s[here, :])
            grads[place][...] = low(grad_s[here, :])


NO_COST = pl.CostEstimate(flops=4_000_000_000, bytes_accessed=4096, transcendentals=0)
ANY = pl.BlockSpec(memory_space=pl.ANY)


def project_blocks(pieces, weight, place, length, before):
    rows, both = pieces[0].shape
    width, wide = weight.shape
    count = len(pieces)
    tall = rows * count
    tile = 256 if wide % 256 == 0 else 128
    return pl.pallas_call(
        functools.partial(project_kernel, count=count),
        grid=(wide // tile,),
        out_shape=[
            jax.ShapeDtypeStruct((length, width), jnp.bfloat16),
            jax.ShapeDtypeStruct((length, wide), jnp.bfloat16),
        ],
        in_specs=[pl.BlockSpec((rows, both), lambda j: (0, 0))] * count
        + [pl.BlockSpec((width, tile), lambda j: (0, j))]
        + [ANY] * len(before),
        out_specs=[
            pl.BlockSpec((tall, width), lambda j: (place, 0)),
            pl.BlockSpec((tall, tile), lambda j: (place, j)),
        ],
        input_output_aliases={count + 1 + i: i for i in range(len(before))},
        compiler_params=pltpu.CompilerParams(vmem_limit_bytes=VMEM_LIMIT),
        cost_estimate=NO_COST,
    )(*pieces, weight, *before)


def feed_blocks(normed, cots, f_in, f_out, place, length, before):
    count = len(normed)
    rows, width = normed[0].shape
    tall, wide = count * rows, f_out.shape[0]
    tile = min(FEED_TILE, wide)
    tiles = wide // tile
    piece = pl.BlockSpec((rows, width), lambda j: (0, 0))
    kept = pl.BlockSpec((tall, width), lambda j: (place, 0))
    part = pl.BlockSpec((tall, tile), lambda j: (place, j))
    outs = pl.pallas_call(
        functools.partial(feed_kernel, count=count),
        grid=(tiles,),
        out_shape=[jax.ShapeDtypeStruct((length, width), jnp.bfloat16)] * 2
        + [jax.ShapeDtypeStruct((length, wide), jnp.bfloat16)] * 3
        + [jax.ShapeDtypeStruct((rows, width), jnp.bfloat16)] * (2 * count),
        in_specs=[piece] * (2 * count)
        + [
            pl.BlockSpec((width, tile), lambda j: (0, j)),
            pl.BlockSpec((width, tile), lambda j: (0, j + tiles)),
            pl.BlockSpec((tile, width), lambda j: (j, 0)),
        ]
        + [ANY] * len(before),
        out_specs=[kept] * 2 + [part] * 3 + [piece] * (2 * count),
        scratch_shapes=[pltpu.VMEM((tall, width), jnp.float32)] * 2,
        input_output_aliases={2 * count + 3 + i: i for i in range(len(before))},
        compiler_params=pltpu.CompilerParams(vmem_limit_bytes=VMEM_LIMIT),
        cost_estimate=NO_COST,
    )(*normed, *cots, f_in, f_in, f_out, *before)
    return outs[:5], outs[5 : 5 + count], outs[5 + count :]


def ring_of(count):
    deep = 4 if count % 4 == 0 else count
    across = count // deep
    ring = [z * across for z in range(deep)]
    for z in reversed(range(deep)):
        turn = range(1, across)
        ring += [z * across + y for y in (turn if (deep - 1 - z) % 2 == 0 else reversed(turn))]
    return ring


class Ring:
    def __init__(self, count):
        self.count = count
        ring = ring_of(count)
        self.ahead = [(ring[p], ring[(p + 1) % count]) for p in range(count)]
        self.behind = [(b, a) for a, b in self.ahead]
        places = [0] * count
        for place, index in enumerate(ring):
            places[index] = place
        places = jnp.array(places, jnp.int32)
        self.slots = [0] * count
        self.slots[count // 2] = 1
        for step in range(1, count // 2):
            self.slots[count - step], self.slots[step] = 2 * step, 2 * step + 1
        here = places[lax.axis_index("blk")]
        self.order = jnp.array(self.slots, jnp.int32)[lax.rem(places - here + count, count)]
        around = lax.rem(jnp.arange(count, dtype=jnp.int32) + here, count)
        self.ahead_index = jnp.array(ring, jnp.int32)[around]

    def forth(self, values):
        return lax.ppermute(values, "blk", self.ahead)

    def back(self, values):
        return lax.ppermute(values, "blk", self.behind)


class Gather:
    def __init__(self, ring, block):
        self.ring = ring
        self.groups = [(block,)]

    def hop(self, *earlier):
        ring, half = self.ring, self.ring.count // 2
        last = self.groups[-1]
        behind, ahead = after((last[0], last[-1]), *earlier)
        if len(self.groups) == half:
            middle = behind.shape[0] // 2
            behind, ahead = behind[:middle], ahead[middle:]
        self.groups.append((ring.forth(behind), ring.back(ahead)))
        return self.groups[-1]

    def place(self, step):
        return {0: 0, self.ring.count // 2: 1}.get(step, step)


class Scatter:
    def __init__(self, ring, partial, axis=0):
        self.ring = ring
        self.partial = partial
        self.axis = axis
        self.step = ring.count // 2
        self.sent = self.moved = self.rider = self.parts = None

    def messages(self, *earlier):
        half, step = self.ring.count // 2, self.step
        self.step -= 1
        if step == half:
            return after(tuple(self.partial(half)), *earlier)
        forward, backward = (part.astype(jnp.float32) for part in after(self.moved, *earlier))
        if step == half - 1:
            extra = forward.shape[self.axis]
            forward = jnp.pad(forward, [(0, extra if axis == self.axis else 0) for axis in (0, 1)])
            backward = jnp.pad(backward, [(extra if axis == self.axis else 0, 0) for axis in (0, 1)])
        parts = self.parts or (self.partial(step), self.partial(self.ring.count - step))
        self.parts = None
        forward, backward = parts[0].astype(jnp.float32) + forward, parts[1].astype(jnp.float32) + backward
        return low(forward), low(backward)

    def compute(self, *earlier):
        self.parts = after((low(self.partial(self.step)), low(self.partial(self.ring.count - self.step))), *earlier)

    def prepare(self, *earlier, rider=None):
        self.sent = self.messages(*earlier)
        self.rider = rider
        if rider is not None:
            self.sent = tuple(
                jnp.concatenate(pair, axis=1) for pair in zip(self.sent, rider.messages(*earlier))
            )
        self.sent = after(self.sent)

    def hop(self, *earlier):
        if self.sent is None:
            self.prepare()
        forward, backward = after(self.sent, *earlier)
        self.moved = (self.ring.forth(forward), self.ring.back(backward))
        self.sent = None

    def hold(self, *others):
        self.moved = after(self.moved, *others)
        if self.rider is not None:
            width = self.partial(0).shape[1]
            self.rider.moved = tuple(part[:, width:] for part in self.moved)
            self.moved = tuple(part[:, :width] for part in self.moved)
            self.rider = None

    def total(self):
        own = self.partial(0).astype(jnp.float32)
        return own + self.moved[0].astype(jnp.float32) + self.moved[1].astype(jnp.float32)


def after(values, *earlier):
    return lax.optimization_barrier((values, earlier))[0]


def sum_axis(values, axis):
    size = lax.axis_size(axis)
    terms = [values] + [
        lax.ppermute(values, axis, [(i, i ^ step) for i in range(size)]) for step in range(1, size)
    ]
    while len(terms) > 1:
        terms = [left + right for left, right in zip(terms[::2], terms[1::2])]
    return terms[0]


def rms_parts(values):
    scale_rows = lax.rsqrt(jnp.mean(values * values, axis=-1, keepdims=True) + EPSILON)
    return (scale_rows, values * scale_rows)


def rms_back(unit_grad, unit, scale_rows):
    return scale_rows * (unit_grad - unit * jnp.mean(unit_grad * unit, axis=-1, keepdims=True))


def sum_over_seq(values, dimension):
    return lax.psum_scatter(low(values), "seq", scatter_dimension=dimension, tiled=True)


def per_device(
    tokens,
    cotangent,
    grouping,
    memory_start,
    normalizer_start,
    gain_attention,
    attention_in,
    gate_logit,
    attention_out,
    gain_feed,
    feed_in,
    feed_out,
):
    rows, width = tokens.shape
    heads_here = memory_start.shape[1]
    count = lax.axis_size("blk")
    ring = Ring(count)
    splits = grouping[0]
    head_first = lax.axis_index("blk") * heads_here
    mix = jax.nn.sigmoid(lax.dynamic_slice_in_dim(gate_logit, head_first, heads_here, 0))

    def whole(weight, axis):
        return lax.all_gather(weight, "seq", axis=axis, tiled=True)

    half = count // 2
    tokens_full = tokens.astype(jnp.float32)
    scale_first, unit_first = rms_parts(tokens_full)

    length = rows * count
    w_in = whole(attention_in.reshape(attention_in.shape[0], -1), 0)
    gather_a = Gather(
        ring, jnp.concatenate([low(unit_first * gain_attention), attention_out.reshape(rows, -1)], axis=1)
    )

    def project(step, kept, *earlier):
        return project_blocks(
            after(gather_a.groups[step], *earlier), w_in, gather_a.place(step), length, kept
        )

    gather_a.hop()
    f_in = whole(after(feed_in, w_in, gather_a.groups[1]).reshape(feed_in.shape[0], -1), 0)
    gather_a.hop()
    kept = project(0, [], gather_a.groups[2])
    for step in range(3, half + 1):
        gather_a.hop(*([kept[1]] if step > 3 else []))
        kept = project(step - 2, kept)
    kept = project(half - 1, kept)
    gather_a.groups[half] = after(gather_a.groups[half], kept[1])
    normed_a, proj = project(half, kept)
    w_out_rows = jnp.zeros((length, gather_a.groups[0][0].shape[1] - width), jnp.bfloat16)
    for step, group in enumerate(gather_a.groups):
        for piece, d, begin in zip(group, (-step % count, step), (0, rows // 2 if step == half else 0)):
            start = ring.ahead_index[d] * rows + begin
            w_out_rows = lax.dynamic_update_slice_in_dim(w_out_rows, piece[:, width:], start, 0)
    w_out = whole(after(w_out_rows.reshape(-1, attention_out.shape[1]), f_in), 1)

    gather_c = Gather(ring, after(cotangent, gather_a.groups[half]))
    gather_c.hop()
    merged, attended, lse, states, norms, memory_final, norm_final = attend_forward(
        ring.order, splits, mix, proj, memory_start[0], normalizer_start[0], rows
    )
    merged_mine = lax.all_to_all(after(merged, gather_c.groups[1]), "blk", 0, 1, tiled=True)
    f_out = whole(after(feed_out, w_out, merged_mine), 1)
    while len(gather_c.groups) < half - 1:
        gather_c.hop(merged_mine)
    middle = tokens_full + dot_nn(merged_mine, w_out)
    scale_second, unit_second = rms_parts(middle)
    gather_f = Gather(ring, after(low(unit_second * gain_feed), gather_c.groups[-1]))
    result_part, normed_f_part = {}, {}
    kept = []

    def feed(step, kept):
        kept, results, grads = feed_blocks(
            gather_f.groups[step], gather_c.groups[step], f_in, f_out, gather_f.place(step), length, kept
        )
        if step == half:
            result_part[half], normed_f_part[half] = results, grads
        else:
            for d, result, grad in zip((-step % count, step), results, grads):
                result_part[d], normed_f_part[d] = result, grad
        return kept

    for step in range(1, half + 1):
        gather_f.hop(gather_c.groups[-1], *kept[2:3])
        if step > 1:
            kept = feed(step - 1 if step < half else half, kept)
        if len(gather_c.groups) <= half:
            gather_c.hop(gather_f.groups[step], *(kept[2:3] if step > 1 else []))
        if step == 1:
            kept = feed(0, kept)
    kept = feed(half - 1, kept)
    normed_f, cot, hidden, gate_grad, up_grad = kept

    scatter_f = Scatter(ring, lambda d: normed_f_part[d])
    for _ in range(half - 2):
        scatter_f.hop()
    feed_out_local = low(dot_tn(hidden, after(cot, scatter_f.moved)))
    scatter_f.hop()
    scatter_f.hold(feed_out_local)
    feed_gate_local = low(dot_tn(normed_f, after(gate_grad, scatter_f.moved)))
    feed_out_grad = sum_over_seq(after(feed_out_local, scatter_f.moved), 1)
    scatter_f.hop()
    scatter_f.hold(feed_gate_local)
    normed_f_grad = scatter_f.total()
    feed_up_local = low(dot_tn(normed_f, after(up_grad, normed_f_grad)))
    scatter_r = Scatter(ring, lambda d: result_part[d])
    scatter_r.hop(normed_f_grad)
    gain_feed_part = jnp.sum(normed_f_grad * unit_second, axis=0)
    middle_grad = cotangent.astype(jnp.float32) + rms_back(
        normed_f_grad * gain_feed, unit_second, scale_second
    )
    out_grad = low(middle_grad)
    combined_grad = after(low(dot_nt(out_grad, w_out)), scatter_r.moved)
    attention_out_local = low(dot_tn(merged_mine, out_grad))
    combined_grad = lax.all_to_all(combined_grad, "blk", 1, 0, tiled=True)
    combined_grad = after(combined_grad, attention_out_local, feed_up_local)
    out_sum = sum_over_seq(after(attention_out_local, feed_out_grad, combined_grad), 1)
    scatter_r.hop(combined_grad)
    proj_grad, gate_rows = attend_backward(
        ring.order, splits, mix, proj, combined_grad,
        attended, lse, states, norms, rows,
    )
    def in_two(values):
        return values[: values.shape[0] // 2], values[values.shape[0] // 2 :]

    def normed_a_part(d):
        first = ring.slots[d] * rows
        if d == half:
            return [low(dot_nt(part, w_in)) for part in in_two(proj_grad[first : first + rows])]
        return dot_nt(proj_grad[first : first + rows], w_in)

    proj_grad = after(proj_grad, scatter_r.moved)
    def attention_out_part(d):
        high = attention_out.shape[0]
        part = lax.dynamic_slice_in_dim(out_sum, ring.ahead_index[d] * high, high, 0).reshape(rows, -1)
        return (part[:, : part.shape[1] // 2], part[:, part.shape[1] // 2 :]) if d == half else part

    scatter_o = Scatter(ring, attention_out_part, axis=1)

    def rider():
        return scatter_o if scatter_o.step > 0 else None

    scatter_a = Scatter(ring, normed_a_part)
    scatter_a.hop()
    scatter_a.hop()
    scatter_r.prepare(proj_grad, rider=rider())
    scatter_a.hold(scatter_r.sent)
    feed_gate_grad = sum_over_seq(after(feed_gate_local, out_sum, scatter_a.moved), 0)
    scatter_r.hop(scatter_a.moved)
    attention_in_local = low(dot_tn(normed_a, after(proj_grad, scatter_a.moved)))
    gain_attention_part = jnp.sum(attention_in_local.astype(jnp.float32) * w_in.astype(jnp.float32), axis=1) / gain_attention
    gate_part = jnp.sum(gate_rows, axis=1) * mix * (1.0 - mix)
    gate_full = lax.dynamic_update_slice_in_dim(
        jnp.zeros(gate_logit.shape, jnp.float32), gate_part, head_first, 0
    )
    sums = jnp.concatenate([gain_attention_part, gain_feed_part, gate_full])
    scatter_a.compute()
    scatter_r.hold(scatter_a.parts, attention_in_local)
    feed_up_grad = sum_over_seq(after(feed_up_local, feed_gate_grad, scatter_r.moved), 0)
    while scatter_a.step > 1:
        scatter_a.prepare(rider=rider())
        scatter_a.hop(scatter_r.moved)
        scatter_a.hold()
        scatter_r.prepare(rider=rider())
        scatter_r.hop(scatter_a.moved)
        scatter_a.compute()
        scatter_r.hold(scatter_a.parts)
    scatter_a.prepare(rider=rider())
    attention_in_grad = sum_over_seq(after(attention_in_local, feed_up_grad, scatter_a.sent), 0)
    sums = sum_axis(after(sums, scatter_a.sent), "seq")
    scatter_a.hop()
    result = low(middle + scatter_r.total())
    feed_in_grad = jnp.stack([feed_gate_grad, feed_up_grad], axis=1).astype(jnp.float32)
    feed_out_grad = feed_out_grad.astype(jnp.float32)
    sums = sum_axis(after(sums, result, feed_in_grad, feed_out_grad), "blk")
    attention_in_grad = attention_in_grad.astype(jnp.float32).reshape(attention_in.shape)
    scatter_a.hold(sums)
    attention_out_grad = scatter_o.total().reshape(attention_out.shape)
    normed_a_grad = scatter_a.total()
    token_grad = middle_grad + rms_back(normed_a_grad * gain_attention, unit_first, scale_first)
    return (
        result,
        token_grad,
        sums[:width],
        attention_in_grad,
        sums[2 * width :],
        attention_out_grad.astype(jnp.float32),
        sums[width : 2 * width],
        feed_in_grad,
        feed_out_grad,
        memory_final[None],
        norm_final[None],
    )


def solution(mesh):
    in_specs = (
        P(("seq", "blk"), None),
        P(("seq", "blk"), None),
        P("seq", None),
        P("seq", "blk", None, None),
        P("seq", "blk", None),
        P(),
        P("seq", None, "blk"),
        P(),
        P("blk", "seq"),
        P(),
        P("seq", None, "blk"),
        P("blk", "seq"),
    )
    out_specs = (
        P(("seq", "blk"), None),
        P(("seq", "blk"), None),
        P(),
        P("seq", None, "blk"),
        P(),
        P("blk", "seq"),
        P(),
        P("seq", None, "blk"),
        P("blk", "seq"),
        P("seq", "blk", None, None),
        P("seq", "blk", None),
    )
    return jax.shard_map(
        per_device, mesh=mesh, in_specs=in_specs, out_specs=out_specs, check_vma=False
    )
```

```python
import functools
import math

import jax
import jax.numpy as jnp
from jax import lax
from jax.experimental import pallas as pl
from jax.experimental.pallas import tpu as pltpu
from jax.sharding import PartitionSpec as P

SHORT = 1024
TILE = 512
FEED_TILE = 256
EPSILON = 1e-06
MASKED = -1e30
LOG2E = math.log2(math.e)
VMEM_LIMIT = 60 * 1024 * 1024


def dot_nn(left, right):
    return lax.dot_general(left, right, (((1,), (0,)), ((), ())), preferred_element_type=jnp.float32)


def dot_nt(left, right):
    return lax.dot_general(left, right, (((1,), (1,)), ((), ())), preferred_element_type=jnp.float32)


def dot_tn(left, right):
    return lax.dot_general(left, right, (((0,), (0,)), ((), ())), preferred_element_type=jnp.float32)


def low(values):
    return values.astype(jnp.bfloat16)


def feature(values):
    return jnp.where(values > 0, values + 1.0, jnp.exp(jnp.minimum(values, 0.0)))


def first_key_tile(index, splits):
    per = 2 * SHORT // TILE
    slot = lax.div(index, per)
    second = (lax.rem(index, per) >= per // 2) & (splits[slot] == 1)
    return slot * per + jnp.where(second, per // 2, 0)


def tile_rows(index):
    return pl.ds(pl.multiple_of(index * TILE, TILE), TILE)


def causal(scores):
    key_pos = lax.broadcasted_iota(jnp.int32, scores.shape, 0)
    query_pos = lax.broadcasted_iota(jnp.int32, scores.shape, 1)
    return jnp.where(key_pos <= query_pos, scores, MASKED)


def state_matrix(memory, norm_row):
    spread = jnp.transpose(jnp.broadcast_to(norm_row, memory.shape))
    return low(jnp.concatenate([memory, spread], axis=1))


def forward_kernel(
    order, splits, mix, proj, memory, norm,
    merged, attended, lse, states, norms, memory_out, norm_out,
    q_s, k_s, v_s, vt_s, *, rows, heads, size,
):
    length = proj.shape[0]
    width = heads * size
    factor = size ** (-0.5) * LOG2E
    for b in range(length // rows):
        src = pl.ds(pl.multiple_of(order[b] * rows, rows), rows)
        dst = slice(b * rows, (b + 1) * rows)
        q_s[dst, :] = proj[src, 0:width]
        k_s[dst, :] = proj[src, width : 2 * width]
        value = proj[src, 2 * width : 3 * width]
        v_s[dst, :] = value
        vt_s[:, dst] = jnp.transpose(value)
    cols = [slice(h * size, (h + 1) * size) for h in range(heads)]

    def query_block(index, _):
        here = tile_rows(index)
        queries = [q_s[here, c] for c in cols]

        def scores_of(tile, h):
            return dot_nt(k_s[tile_rows(tile), cols[h]], queries[h]) * factor

        def weigh(tile, h, scores, highest):
            weights = jnp.exp2(scores - highest)
            total = jnp.sum(weights, axis=0, keepdims=True)
            return total, dot_nn(vt_s[cols[h], tile_rows(tile)], low(weights))

        start = []
        for h in range(heads):
            scores = causal(scores_of(index, h))
            highest = jnp.max(scores, axis=0, keepdims=True)
            start.append((highest, *weigh(index, h, scores, highest)))

        def step(tile, carry):
            out = []
            for h in range(heads):
                highest, total, acc = carry[h]
                scores = scores_of(tile, h)
                higher = jnp.maximum(highest, jnp.max(scores, axis=0, keepdims=True))
                keep = jnp.exp2(highest - higher)
                more, add = weigh(tile, h, scores, higher)
                out.append((higher, total * keep + more, acc * keep + add))
            return tuple(out)

        done = lax.fori_loop(first_key_tile(index, splits), index, step, tuple(start))
        for h in range(heads):
            highest, total, acc = done[h]
            attended[here, cols[h]] = jnp.transpose(acc / total)
            lse[index, h : h + 1, :] = highest + jnp.log2(total)
        return 0

    lax.fori_loop(0, length // TILE, query_block, 0)

    for h in range(heads):
        total_m, total_n = memory[h], norm[h : h + 1, :]
        now_m, now_n = total_m, total_n
        share = mix[h]
        for half in range(length // SHORT):
            fresh = True if half % 2 == 0 else splits[half // 2] == 1
            now_m = jnp.where(fresh, total_m, now_m)
            now_n = jnp.where(fresh, total_n, now_n)
            states[half, h] = now_m
            norms[half, h : h + 1, :] = now_n
            both = state_matrix(now_m, now_n)

            def chunk(index, carry):
                here = tile_rows(index)
                grown_m, grown_n = carry
                query_feat = feature(q_s[here, cols[h]].astype(jnp.float32))
                key_feat = feature(k_s[here, cols[h]].astype(jnp.float32))
                read = dot_nn(low(query_feat), both)
                recalled = read[:, :size] / read[:, size:]
                merged[here, cols[h]] = low(share * recalled + (1.0 - share) * attended[here, cols[h]])
                back = dot_nn(low(key_feat), both)
                miss = v_s[here, cols[h]].astype(jnp.float32) - back[:, :size] / back[:, size:]
                return (
                    grown_m + dot_tn(low(key_feat), low(miss)),
                    grown_n + jnp.sum(key_feat, axis=0, keepdims=True),
                )

            per = SHORT // TILE
            total_m, total_n = lax.fori_loop(half * per, (half + 1) * per, chunk, (total_m, total_n))
        memory_out[h] = total_m
        norm_out[h : h + 1, :] = total_n


def backward_kernel(
    order, splits, mix, proj, combined_grad, attended, lse, states, norms,
    proj_grad, gate,
    q_s, k_s, v_s, kt_s, g_s, delta_s, dq_s, dk_s, dv_s, *, rows, heads, size,
):
    length = proj.shape[0]
    width = heads * size
    scale = size ** (-0.5)
    factor = scale * LOG2E
    for b in range(length // rows):
        src = pl.ds(pl.multiple_of(order[b] * rows, rows), rows)
        dst = slice(b * rows, (b + 1) * rows)
        q_s[dst, :] = proj[src, 0:width]
        key = proj[src, width : 2 * width]
        k_s[dst, :] = key
        v_s[dst, :] = proj[src, 2 * width : 3 * width]
        kt_s[:, dst] = jnp.transpose(key)
    cols = [slice(h * size, (h + 1) * size) for h in range(heads)]
    ones = jnp.ones((8, size), jnp.float32)
    slots = length // (2 * SHORT)
    per = SHORT // TILE

    for h in range(heads):
        share = mix[h]
        col = cols[h]
        gate_sum = jnp.zeros((1, size), jnp.float32)
        next_m, next_n = jnp.zeros((size, size), jnp.float32), jnp.zeros((1, size), jnp.float32)
        for slot in reversed(range(slots)):
            split = splits[slot] == 1
            later_m, later_n = None, None
            for half in (2 * slot + 1, 2 * slot):
                last = half == 2 * slots - 1
                if half % 2 == 1:
                    up_m, up_n = next_m, next_n
                else:
                    up_m = jnp.where(split, later_m, next_m)
                    up_n = jnp.where(split, later_n, next_n)
                memory = states[half, h]
                norm_row = norms[half, h : h + 1, :]
                both = state_matrix(memory, norm_row)
                low_memory = low(memory)
                low_up = low(up_m)
                up_both = jnp.concatenate([low_up, low_memory], axis=1)

                def chunk(index, carry, both=both, low_memory=low_memory, low_up=low_up, up_both=up_both, norm_row=norm_row, up_n=up_n, last=last):
                    here = tile_rows(index)
                    sum_m, sum_n, sum_gate = carry
                    att = attended[here, col]
                    grad = combined_grad[here, col].astype(jnp.float32)
                    query_feat = feature(q_s[here, col].astype(jnp.float32))
                    read = dot_nn(low(query_feat), both)
                    inverse = 1.0 / read[:, size:]
                    recalled = read[:, :size] * inverse
                    recalled_grad = share * grad
                    attended_grad = low((1.0 - share) * grad)
                    g_s[here, col] = attended_grad
                    sums = lax.dot_general(
                        ones, attended_grad.astype(jnp.float32) * att, (((1,), (1,)), ((), ())),
                        precision=lax.Precision.HIGHEST, preferred_element_type=jnp.float32,
                    )
                    delta_s[index, h : h + 1, :] = sums[0:1, :]
                    sum_gate = sum_gate + jnp.sum(grad * (recalled - att), axis=0, keepdims=True)
                    scaled = recalled_grad * inverse
                    den_grad = -jnp.sum(recalled_grad * recalled, axis=1, keepdims=True) * inverse
                    query_feat_grad = dot_nt(low(scaled), low_memory) + den_grad * norm_row
                    dq_s[here, col] = query_feat_grad * jnp.minimum(query_feat, 1.0)
                    sum_m = sum_m + dot_tn(low(query_feat), low(scaled))
                    sum_n = sum_n + jnp.sum(den_grad * query_feat, axis=0, keepdims=True)
                    if last:
                        dk_s[here, col] = jnp.zeros((TILE, size), jnp.float32)
                        dv_s[here, col] = jnp.zeros((TILE, size), jnp.float32)
                    else:
                        key_feat = feature(k_s[here, col].astype(jnp.float32))
                        back = dot_nn(low(key_feat), both)
                        key_inverse = 1.0 / back[:, size:]
                        retrieved = back[:, :size] * key_inverse
                        miss = v_s[here, col].astype(jnp.float32) - retrieved
                        miss_grad = dot_nn(low(key_feat), low_up)
                        dv_s[here, col] = miss_grad
                        pair = jnp.concatenate([low(miss), low(-miss_grad * key_inverse)], axis=1)
                        along = jnp.sum(miss_grad * retrieved, axis=1, keepdims=True) * key_inverse
                        key_feat_grad = dot_nt(pair, up_both) + along * norm_row + up_n
                        dk_s[here, col] = key_feat_grad * jnp.minimum(key_feat, 1.0)
                    return sum_m, sum_n, sum_gate

                sum_m, sum_n, gate_sum = lax.fori_loop(
                    half * per, (half + 1) * per, chunk,
                    (jnp.zeros((size, size), jnp.float32), jnp.zeros((1, size), jnp.float32), gate_sum),
                )
                if half % 2 == 1:
                    later_m, later_n = sum_m, sum_n
                else:
                    next_m = jnp.where(split, sum_m, sum_m + later_m)
                    next_n = jnp.where(split, sum_n, sum_n + later_n)
        gate[h : h + 1, :] = gate_sum

    def query_block(index, _):
        here = tile_rows(index)

        def part(tile, h, mask):
            there = tile_rows(tile)
            col = cols[h]
            queries, grads, keys = q_s[here, col], g_s[here, col], k_s[there, col]
            scores = dot_nt(keys, queries) * factor
            if mask:
                scores = causal(scores)
            probs = jnp.exp2(scores - lse[index, h : h + 1, :])
            prob_grad = dot_nt(v_s[there, col], grads)
            score_grad = low(probs * (prob_grad - delta_s[index, h : h + 1, :]))
            dv_s[there, col] += dot_nn(low(probs), grads)
            dk_s[there, col] += dot_nn(score_grad, queries) * scale
            return dot_nn(kt_s[col, there], score_grad)

        start = tuple(part(index, h, True) for h in range(heads))

        def step(tile, carry):
            return tuple(carry[h] + part(tile, h, False) for h in range(heads))

        done = lax.fori_loop(first_key_tile(index, splits), index, step, start)
        for h in range(heads):
            dq_s[here, cols[h]] += jnp.transpose(done[h]) * scale
        return 0

    lax.fori_loop(0, length // TILE, query_block, 0)
    for b in range(length // rows):
        dst = pl.ds(pl.multiple_of(order[b] * rows, rows), rows)
        src = slice(b * rows, (b + 1) * rows)
        proj_grad[dst, 0:width] = low(dq_s[src, :])
        proj_grad[dst, width : 2 * width] = low(dk_s[src, :])
        proj_grad[dst, 2 * width : 3 * width] = low(dv_s[src, :])


SMEM = pl.BlockSpec(memory_space=pltpu.SMEM)
VMEM = pl.BlockSpec(memory_space=pltpu.VMEM)


def attend_forward(order, splits, mix, proj, memory, norm, rows):
    heads, size, _ = memory.shape
    length, width = proj.shape[0], heads * size
    halves, tiles = length // SHORT, length // TILE
    shapes = [
        jax.ShapeDtypeStruct((length, width), jnp.bfloat16),
        jax.ShapeDtypeStruct((length, width), jnp.float32),
        jax.ShapeDtypeStruct((tiles, heads, TILE), jnp.float32),
        jax.ShapeDtypeStruct((halves, heads, size, size), jnp.float32),
        jax.ShapeDtypeStruct((halves, heads, size), jnp.float32),
        jax.ShapeDtypeStruct((heads, size, size), jnp.float32),
        jax.ShapeDtypeStruct((heads, size), jnp.float32),
    ]
    whole = pltpu.VMEM((length, width), jnp.bfloat16)
    return pl.pallas_call(
        functools.partial(forward_kernel, rows=rows, heads=heads, size=size),
        out_shape=shapes,
        in_specs=[SMEM] * 3 + [VMEM] * 3,
        out_specs=[VMEM] * len(shapes),
        scratch_shapes=[whole, whole, whole, pltpu.VMEM((width, length), jnp.bfloat16)],
        compiler_params=pltpu.CompilerParams(vmem_limit_bytes=VMEM_LIMIT),
        cost_estimate=NO_COST,
    )(order, splits, mix, proj, memory, norm)


def attend_backward(order, splits, mix, proj, combined_grad, attended, lse, states, norms, rows):
    _, heads, size, _ = states.shape
    length, width = proj.shape[0], heads * size
    tiles = length // TILE
    shapes = [
        jax.ShapeDtypeStruct((length, 3 * width), jnp.bfloat16),
        jax.ShapeDtypeStruct((heads, size), jnp.float32),
    ]
    whole = pltpu.VMEM((length, width), jnp.bfloat16)
    wide = pltpu.VMEM((length, width), jnp.float32)
    return pl.pallas_call(
        functools.partial(backward_kernel, rows=rows, heads=heads, size=size),
        out_shape=shapes,
        in_specs=[SMEM] * 3 + [VMEM] * 6,
        out_specs=[VMEM] * len(shapes),
        scratch_shapes=[
            whole, whole, whole, pltpu.VMEM((width, length), jnp.bfloat16), whole,
            pltpu.VMEM((tiles, heads, TILE), jnp.float32), wide, wide, wide,
        ],
        compiler_params=pltpu.CompilerParams(vmem_limit_bytes=VMEM_LIMIT),
        cost_estimate=NO_COST,
    )(order, splits, mix, proj, combined_grad, attended, lse, states, norms)


def fill(whole, pieces):
    rows = pieces[0].shape[0]
    for place, piece in enumerate(pieces):
        whole[place * rows : (place + 1) * rows, :] = piece[...]


def project_kernel(*refs, count):
    pieces, weight = refs[:count], refs[count]
    normed_all, extra_all, proj_all = refs[-3:]
    width = normed_all.shape[1]

    @pl.when(pl.program_id(0) == 0)
    def _():
        begin = 0
        for piece in pieces:
            here = slice(begin, begin + piece.shape[0])
            normed_all[here, :] = piece[:, :width]
            extra_all[here, :] = piece[:, width:]
            begin += piece.shape[0]

    proj_all[...] = low(dot_nn(normed_all[...], weight[...]))


def widen_kernel(*refs):
    out, parts = refs[-1], refs[:-1]
    columns = out.shape[2]
    place = 0
    for part in parts:
        for begin in range(0, part.shape[1], columns):
            out[:, place, :] = part[:, begin : begin + columns].astype(jnp.float32)
            place += 1


def widen(parts, shape):
    rows = shape[0]
    tall = min(rows, 128)
    return pl.pallas_call(
        widen_kernel,
        grid=(rows // tall,),
        out_shape=jax.ShapeDtypeStruct(shape, jnp.float32),
        in_specs=[pl.BlockSpec((tall, part.shape[1]), lambda i: (i, 0)) for part in parts],
        out_specs=pl.BlockSpec((tall, *shape[1:]), lambda i: (i, 0, 0)),
        cost_estimate=NO_COST,
    )(*parts)


def feed_kernel(*refs, count):
    normed, cots = refs[:count], refs[count : 2 * count]
    w_gate, w_up, w_down = refs[2 * count : 2 * count + 3]
    result_s, grad_s = refs[-2:]
    results, grads = refs[-2 - 2 * count : -2 - count], refs[-2 - count : -2]
    normed_all, cot_all, hidden, gate_grad, up_grad = refs[-7 - 2 * count : -2 - 2 * count]
    step = pl.program_id(0)

    @pl.when(step == 0)
    def _():
        fill(normed_all, normed)
        fill(cot_all, cots)

    gate = dot_nn(normed_all[...], w_gate[...])
    up = dot_nn(normed_all[...], w_up[...])
    hidden_grad = dot_nt(cot_all[...], w_down[...])
    sigmoid_gate = 1.0 / (1.0 + jnp.exp(-gate))
    activated = gate * sigmoid_gate
    low_hidden = low(activated * up)
    low_gate = low(hidden_grad * up * (sigmoid_gate + activated * (1.0 - sigmoid_gate)))
    low_up = low(hidden_grad * activated)
    hidden[...] = low_hidden
    gate_grad[...] = low_gate
    up_grad[...] = low_up
    more_result = dot_nn(low_hidden, w_down[...])
    more_grad = dot_nt(low_gate, w_gate[...]) + dot_nt(low_up, w_up[...])

    @pl.when(step == 0)
    def _():
        result_s[...] = more_result
        grad_s[...] = more_grad

    @pl.when(step > 0)
    def _():
        result_s[...] += more_result
        grad_s[...] += more_grad

    @pl.when(step == pl.num_programs(0) - 1)
    def _():
        rows = results[0].shape[0]
        for place in range(count):
            here = slice(place * rows, (place + 1) * rows)
            results[place][...] = low(result_s[here, :])
            grads[place][...] = low(grad_s[here, :])


NO_COST = pl.CostEstimate(flops=4_000_000_000, bytes_accessed=4096, transcendentals=0)
ANY = pl.BlockSpec(memory_space=pl.ANY)


def project_blocks(pieces, weight, place, length, before):
    both = pieces[0].shape[1]
    width, wide = weight.shape
    count = len(pieces)
    tall = sum(piece.shape[0] for piece in pieces)
    tile = 256 if wide % 256 == 0 else 128
    return pl.pallas_call(
        functools.partial(project_kernel, count=count),
        grid=(wide // tile,),
        out_shape=[
            jax.ShapeDtypeStruct((length, width), jnp.bfloat16),
            jax.ShapeDtypeStruct((length, both - width), jnp.bfloat16),
            jax.ShapeDtypeStruct((length, wide), jnp.bfloat16),
        ],
        in_specs=[pl.BlockSpec(piece.shape, lambda j: (0, 0)) for piece in pieces]
        + [pl.BlockSpec((width, tile), lambda j: (0, j))]
        + [ANY] * len(before),
        out_specs=[
            pl.BlockSpec((tall, width), lambda j: (place, 0)),
            pl.BlockSpec((tall, both - width), lambda j: (place, 0)),
            pl.BlockSpec((tall, tile), lambda j: (place, j)),
        ],
        input_output_aliases={count + 1 + i: i for i in range(len(before))},
        compiler_params=pltpu.CompilerParams(vmem_limit_bytes=VMEM_LIMIT),
        cost_estimate=NO_COST,
    )(*pieces, weight, *before)


def feed_blocks(normed, cots, f_in, f_out, place, length, before):
    count = len(normed)
    rows, width = normed[0].shape
    tall, wide = count * rows, f_out.shape[0]
    tile = min(FEED_TILE, wide)
    tiles = wide // tile
    piece = pl.BlockSpec((rows, width), lambda j: (0, 0))
    kept = pl.BlockSpec((tall, width), lambda j: (place, 0))
    part = pl.BlockSpec((tall, tile), lambda j: (place, j))
    outs = pl.pallas_call(
        functools.partial(feed_kernel, count=count),
        grid=(tiles,),
        out_shape=[jax.ShapeDtypeStruct((length, width), jnp.bfloat16)] * 2
        + [jax.ShapeDtypeStruct((length, wide), jnp.bfloat16)] * 3
        + [jax.ShapeDtypeStruct((rows, width), jnp.bfloat16)] * (2 * count),
        in_specs=[piece] * (2 * count)
        + [
            pl.BlockSpec((width, tile), lambda j: (0, j)),
            pl.BlockSpec((width, tile), lambda j: (0, j + tiles)),
            pl.BlockSpec((tile, width), lambda j: (j, 0)),
        ]
        + [ANY] * len(before),
        out_specs=[kept] * 2 + [part] * 3 + [piece] * (2 * count),
        scratch_shapes=[pltpu.VMEM((tall, width), jnp.float32)] * 2,
        input_output_aliases={2 * count + 3 + i: i for i in range(len(before))},
        compiler_params=pltpu.CompilerParams(vmem_limit_bytes=VMEM_LIMIT),
        cost_estimate=NO_COST,
    )(*normed, *cots, f_in, f_in, f_out, *before)
    return outs[:5], outs[5 : 5 + count], outs[5 + count :]


def ring_of(count):
    deep = 4 if count % 4 == 0 else count
    across = count // deep
    ring = [z * across for z in range(deep)]
    for z in reversed(range(deep)):
        turn = range(1, across)
        ring += [z * across + y for y in (turn if (deep - 1 - z) % 2 == 0 else reversed(turn))]
    return ring


class Ring:
    def __init__(self, count):
        self.count = count
        ring = ring_of(count)
        self.ahead = [(ring[p], ring[(p + 1) % count]) for p in range(count)]
        self.behind = [(b, a) for a, b in self.ahead]
        places = [0] * count
        for place, index in enumerate(ring):
            places[index] = place
        places = jnp.array(places, jnp.int32)
        self.slots = [0] * count
        self.slots[count // 2] = 1
        for step in range(1, count // 2):
            self.slots[count - step], self.slots[step] = 2 * step, 2 * step + 1
        here = places[lax.axis_index("blk")]
        self.order = jnp.array(self.slots, jnp.int32)[lax.rem(places - here + count, count)]
        around = lax.rem(jnp.arange(count, dtype=jnp.int32) + here, count)
        self.ahead_index = jnp.array(ring, jnp.int32)[around]

    def forth(self, values):
        return lax.ppermute(values, "blk", self.ahead)

    def back(self, values):
        return lax.ppermute(values, "blk", self.behind)


class Gather:
    def __init__(self, ring, block):
        self.ring = ring
        self.groups = [(block,)]

    def hop(self, *earlier):
        ring, half = self.ring, self.ring.count // 2
        last = self.groups[-1]
        behind, ahead = after((last[0], last[-1]), *earlier)
        if len(self.groups) == half:
            middle = behind.shape[0] // 2
            behind, ahead = behind[:middle], ahead[middle:]
        self.groups.append((ring.forth(behind), ring.back(ahead)))
        return self.groups[-1]

    def place(self, step):
        return {0: 0, self.ring.count // 2: 1}.get(step, step)


class Scatter:
    def __init__(self, ring, partial, axis=0):
        self.ring = ring
        self.partial = partial
        self.axis = axis
        self.step = ring.count // 2
        self.sent = self.moved = self.rider = self.parts = None
        self.begin = 0
        self.fresh = True

    def messages(self, *earlier):
        half, step = self.ring.count // 2, self.step
        self.step -= 1
        if step == half:
            return after(tuple(self.partial(half)), *earlier)
        forward, backward = self.came(*earlier)
        if step == half - 1:
            extra = forward.shape[self.axis]
            forward = jnp.pad(forward, [(0, extra if axis == self.axis else 0) for axis in (0, 1)])
            backward = jnp.pad(backward, [(extra if axis == self.axis else 0, 0) for axis in (0, 1)])
        parts = self.parts or (self.partial(step), self.partial(self.ring.count - step))
        self.parts = None
        forward, backward = parts[0].astype(jnp.float32) + forward, parts[1].astype(jnp.float32) + backward
        return low(forward), low(backward)

    def compute(self, *earlier):
        self.parts = after((low(self.partial(self.step)), low(self.partial(self.ring.count - self.step))), *earlier)

    def came(self, *earlier):
        width = self.partial(0).shape[1]
        return [
            part[:, self.begin : self.begin + width].astype(jnp.float32) for part in after(self.moved, *earlier)
        ]

    def prepare(self, *earlier, rider=None):
        self.sent = self.messages(*earlier)
        self.fresh = False
        self.rider = rider
        if rider is not None:
            self.sent = tuple(
                jnp.concatenate(pair, axis=1) for pair in zip(self.sent, rider.messages(*earlier))
            )
        self.sent = after(self.sent)

    def hop(self, *earlier):
        if self.fresh:
            self.prepare()
        self.fresh = True
        forward, backward = self.sent = after(self.sent, *earlier)
        self.moved = (self.ring.forth(forward), self.ring.back(backward))

    def hold(self, *others):
        self.moved = after(self.moved, *others)
        if self.rider is not None:
            self.rider.moved, self.rider.begin = self.moved, self.partial(0).shape[1]
            self.rider = None

    def total(self):
        forward, backward = self.came()
        return self.partial(0).astype(jnp.float32) + forward + backward


def after(values, *earlier):
    return lax.optimization_barrier((values, earlier))[0]


def sum_axis(values, axis):
    size = lax.axis_size(axis)
    terms = [values] + [
        lax.ppermute(values, axis, [(i, i ^ step) for i in range(size)]) for step in range(1, size)
    ]
    while len(terms) > 1:
        terms = [left + right for left, right in zip(terms[::2], terms[1::2])]
    return terms[0]


def swap_sum(values, axis, step, *earlier):
    size = lax.axis_size(axis)
    return values + after(lax.ppermute(values, axis, [(i, i ^ step) for i in range(size)]), *earlier)


def rms_parts(values):
    scale_rows = lax.rsqrt(jnp.mean(values * values, axis=-1, keepdims=True) + EPSILON)
    return (scale_rows, values * scale_rows)


def rms_back(unit_grad, unit, scale_rows):
    return scale_rows * (unit_grad - unit * jnp.mean(unit_grad * unit, axis=-1, keepdims=True))


def sum_over_seq(values, dimension):
    return lax.psum_scatter(low(values), "seq", scatter_dimension=dimension, tiled=True)


def per_device(
    tokens,
    cotangent,
    grouping,
    memory_start,
    normalizer_start,
    gain_attention,
    attention_in,
    gate_logit,
    attention_out,
    gain_feed,
    feed_in,
    feed_out,
):
    rows, width = tokens.shape
    heads_here = memory_start.shape[1]
    count = lax.axis_size("blk")
    ring = Ring(count)
    splits = grouping[0]
    head_first = lax.axis_index("blk") * heads_here
    mix = jax.nn.sigmoid(lax.dynamic_slice_in_dim(gate_logit, head_first, heads_here, 0))

    def whole(weight, axis):
        return lax.all_gather(weight, "seq", axis=axis, tiled=True)

    half = count // 2
    tokens_full = tokens.astype(jnp.float32)
    scale_first, unit_first = rms_parts(tokens_full)

    length = rows * count
    w_in = whole(attention_in.reshape(attention_in.shape[0], -1), 0)
    gather_a = Gather(
        ring, jnp.concatenate([low(unit_first * gain_attention), attention_out.reshape(rows, -1)], axis=1)
    )

    gather_a.hop()
    f_in = whole(after(feed_in, w_in, gather_a.groups[1]).reshape(feed_in.shape[0], -1), 0)
    kept = []
    for step in range(2, half + 1):
        gather_a.hop(*kept[2:3])
        if step > 2:
            kept = project_blocks(gather_a.groups[step - 2], w_in, step - 2, length, kept)
    kept = project_blocks(gather_a.groups[half - 1], w_in, half - 1, length, kept)
    gather_a.groups[half] = after(gather_a.groups[half], kept[2])
    normed_a, extra, proj = project_blocks(gather_a.groups[0] + gather_a.groups[half], w_in, 0, length, kept)
    extra = extra.reshape(count, *attention_out.shape)[ring.order].reshape(-1, attention_out.shape[1])
    w_out = whole(after(extra, f_in), 1)

    gather_c = Gather(ring, after(cotangent, gather_a.groups[half]))
    gather_c.hop()
    merged, attended, lse, states, norms, memory_final, norm_final = attend_forward(
        ring.order, splits, mix, proj, memory_start[0], normalizer_start[0], rows
    )
    merged_mine = lax.all_to_all(after(merged, gather_c.groups[1]), "blk", 0, 1, tiled=True)
    f_out = whole(after(feed_out, w_out, merged_mine), 1)
    while len(gather_c.groups) < half - 1:
        gather_c.hop(merged_mine)
    middle = tokens_full + dot_nn(merged_mine, w_out)
    scale_second, unit_second = rms_parts(middle)
    gather_f = Gather(ring, after(low(unit_second * gain_feed), gather_c.groups[-1]))
    result_part, normed_f_part = {}, {}
    kept = []

    def feed(step, kept):
        kept, results, grads = feed_blocks(
            gather_f.groups[step], gather_c.groups[step], f_in, f_out, gather_f.place(step), length, kept
        )
        if step == half:
            result_part[half], normed_f_part[half] = results, grads
        else:
            for d, result, grad in zip((-step % count, step), results, grads):
                result_part[d], normed_f_part[d] = result, grad
        return kept

    for step in range(1, half + 1):
        gather_f.hop(gather_c.groups[-1], *kept[2:3])
        if step > 1:
            kept = feed(step - 1 if step < half else half, kept)
        if len(gather_c.groups) <= half:
            gather_c.hop(gather_f.groups[step], *(kept[2:3] if step > 1 else []))
        if step == 1:
            kept = feed(0, kept)
    kept = feed(half - 1, kept)
    normed_f, cot, hidden, gate_grad, up_grad = kept

    scatter_f = Scatter(ring, lambda d: normed_f_part[d])
    scatter_r = Scatter(ring, lambda d: result_part[d])
    scatter_f.hop()
    scatter_r.hop(scatter_f.sent)
    scatter_f.hop(scatter_r.moved)
    for _ in range(half - 4):
        scatter_f.hop()
    feed_out_local = low(dot_tn(hidden, after(cot, scatter_f.sent)))
    scatter_f.hold(feed_out_local)
    feed_out_grad = sum_over_seq(after(feed_out_local, scatter_f.moved), 1)
    scatter_f.hop()
    feed_gate_local = low(dot_tn(normed_f, after(gate_grad, scatter_f.sent)))
    scatter_f.hold(feed_gate_local)
    scatter_f.hop()
    feed_up_local = low(dot_tn(normed_f, after(up_grad, scatter_f.sent)))
    scatter_f.hold(feed_up_local)
    normed_f_grad = scatter_f.total()
    feed_gate_grad = sum_over_seq(after(feed_gate_local, feed_out_grad, normed_f_grad), 0)
    scatter_r.prepare()
    gain_feed_part = jnp.sum(normed_f_grad * unit_second, axis=0)
    middle_grad = cotangent.astype(jnp.float32) + rms_back(
        normed_f_grad * gain_feed, unit_second, scale_second
    )
    out_grad = low(middle_grad)
    combined_grad = low(dot_nt(out_grad, w_out))
    attention_out_local = low(dot_tn(merged_mine, after(out_grad, feed_up_local)))
    combined_grad = lax.all_to_all(combined_grad, "blk", 1, 0, tiled=True)
    combined_grad = after(combined_grad, attention_out_local, scatter_r.sent)
    out_sum = sum_over_seq(after(attention_out_local, feed_gate_grad, combined_grad), 1)
    scatter_r.hop(combined_grad)
    proj_grad, gate_rows = attend_backward(
        ring.order, splits, mix, proj, combined_grad,
        attended, lse, states, norms, rows,
    )
    def in_two(values):
        return values[: values.shape[0] // 2], values[values.shape[0] // 2 :]

    def normed_a_part(d):
        first = ring.slots[d] * rows
        if d == half:
            return [low(dot_nt(part, w_in)) for part in in_two(proj_grad[first : first + rows])]
        return dot_nt(proj_grad[first : first + rows], w_in)

    proj_grad = after(proj_grad, scatter_r.moved)
    def attention_out_part(d):
        high = attention_out.shape[0]
        part = lax.dynamic_slice_in_dim(out_sum, ring.ahead_index[d] * high, high, 0).reshape(rows, -1)
        return (part[:, : part.shape[1] // 2], part[:, part.shape[1] // 2 :]) if d == half else part

    scatter_o = Scatter(ring, attention_out_part, axis=1)

    def rider():
        return scatter_o if scatter_o.step > 0 else None

    scatter_a = Scatter(ring, normed_a_part)
    scatter_a.hop()
    scatter_a.compute(scatter_a.sent)
    scatter_a.hold(scatter_a.parts)
    scatter_a.hop()
    scatter_r.prepare(scatter_a.sent, rider=rider())
    scatter_a.hold(scatter_r.sent)
    feed_up_grad = sum_over_seq(after(feed_up_local, out_sum, scatter_a.moved), 0)
    scatter_r.hop(scatter_a.moved)
    attention_in_local = low(dot_tn(normed_a, after(proj_grad, scatter_a.moved)))
    gain_attention_part = jnp.sum(attention_in_local.astype(jnp.float32) * w_in.astype(jnp.float32), axis=1) / gain_attention
    gate_part = jnp.sum(gate_rows, axis=1) * mix * (1.0 - mix)
    gate_full = lax.dynamic_update_slice_in_dim(
        jnp.zeros(gate_logit.shape, jnp.float32), gate_part, head_first, 0
    )
    sums = jnp.concatenate([gain_attention_part, gain_feed_part, gate_full])
    scatter_a.compute(scatter_a.moved)
    sums = sum_axis(sums, "seq")
    scatter_r.hold(scatter_a.parts, attention_in_local, sums)
    swaps = [1 << bit for bit in range(count.bit_length() - 1)]
    while scatter_a.step > 1:
        scatter_a.prepare(rider=rider())
        scatter_a.hop(scatter_r.moved)
        if swaps:
            sums = swap_sum(after(sums, scatter_a.sent), "blk", swaps.pop())
        scatter_a.hold(sums)
        scatter_r.prepare(rider=rider())
        scatter_r.hop(scatter_a.moved)
        scatter_a.compute(scatter_r.sent)
        if swaps:
            sums = swap_sum(after(sums, scatter_r.sent), "blk", swaps.pop())
        scatter_r.hold(scatter_a.parts, sums)
    scatter_a.prepare(rider=rider())
    attention_in_grad = sum_over_seq(after(attention_in_local, feed_up_grad, scatter_a.sent), 0)
    scatter_a.hop()
    sums = after(sums, scatter_a.sent)
    while len(swaps) > 1:
        sums = swap_sum(sums, "blk", swaps.pop())
    feed_in_grad = widen(after((feed_gate_grad, feed_up_grad), scatter_a.sent), feed_in.shape)
    result, feed_out_grad = after((low(middle + scatter_r.total()), feed_out_grad), scatter_a.sent)
    feed_out_grad = feed_out_grad.astype(jnp.float32)
    attention_in_grad = widen((attention_in_grad,), attention_in.shape)
    while swaps:
        sums = swap_sum(sums, "blk", swaps.pop(), result, feed_in_grad, feed_out_grad, attention_in_grad)
    scatter_a.hold(sums)
    attention_out_grad = scatter_o.total().reshape(attention_out.shape)
    normed_a_grad = scatter_a.total()
    token_grad = middle_grad + rms_back(normed_a_grad * gain_attention, unit_first, scale_first)
    return (
        result,
        token_grad,
        sums[:width],
        attention_in_grad,
        sums[2 * width :],
        attention_out_grad.astype(jnp.float32),
        sums[width : 2 * width],
        feed_in_grad,
        feed_out_grad,
        memory_final[None],
        norm_final[None],
    )


def solution(mesh):
    in_specs = (
        P(("seq", "blk"), None),
        P(("seq", "blk"), None),
        P("seq", None),
        P("seq", "blk", None, None),
        P("seq", "blk", None),
        P(),
        P("seq", None, "blk"),
        P(),
        P("blk", "seq"),
        P(),
        P("seq", None, "blk"),
        P("blk", "seq"),
    )
    out_specs = (
        P(("seq", "blk"), None),
        P(("seq", "blk"), None),
        P(),
        P("seq", None, "blk"),
        P(),
        P("blk", "seq"),
        P(),
        P("seq", None, "blk"),
        P("blk", "seq"),
        P("seq", "blk", None, None),
        P("seq", "blk", None),
    )
    return jax.shard_map(
        per_device, mesh=mesh, in_specs=in_specs, out_specs=out_specs, check_vma=False
    )
```

```python
import functools
import math

import jax
import jax.numpy as jnp
from jax import lax
from jax.experimental import pallas as pl
from jax.experimental.pallas import tpu as pltpu
from jax.sharding import PartitionSpec as P

SHORT = 1024
TILE = 512
FEED_TILE = 256
EPSILON = 1e-06
MASKED = -1e30
LOG2E = math.log2(math.e)
VMEM_LIMIT = 60 * 1024 * 1024


def dot_nn(left, right):
    return lax.dot_general(left, right, (((1,), (0,)), ((), ())), preferred_element_type=jnp.float32)


def dot_nt(left, right):
    return lax.dot_general(left, right, (((1,), (1,)), ((), ())), preferred_element_type=jnp.float32)


def dot_tn(left, right):
    return lax.dot_general(left, right, (((0,), (0,)), ((), ())), preferred_element_type=jnp.float32)


def low(values):
    return values.astype(jnp.bfloat16)


def feature(values):
    return jnp.where(values > 0, values + 1.0, jnp.exp(jnp.minimum(values, 0.0)))


def first_key_tile(index, splits):
    per = 2 * SHORT // TILE
    slot = lax.div(index, per)
    second = (lax.rem(index, per) >= per // 2) & (splits[slot] == 1)
    return slot * per + jnp.where(second, per // 2, 0)


def tile_rows(index):
    return pl.ds(pl.multiple_of(index * TILE, TILE), TILE)


def causal(scores):
    key_pos = lax.broadcasted_iota(jnp.int32, scores.shape, 0)
    query_pos = lax.broadcasted_iota(jnp.int32, scores.shape, 1)
    return jnp.where(key_pos <= query_pos, scores, MASKED)


def state_matrix(memory, norm_row):
    spread = jnp.transpose(jnp.broadcast_to(norm_row, memory.shape))
    return low(jnp.concatenate([memory, spread], axis=1))


def forward_kernel(
    order, splits, mix, proj, memory, norm,
    merged, attended, lse, states, norms, memory_out, norm_out,
    q_s, k_s, v_s, vt_s, *, rows, heads, size,
):
    length = proj.shape[0]
    width = heads * size
    factor = size ** (-0.5) * LOG2E
    for b in range(length // rows):
        src = pl.ds(pl.multiple_of(order[b] * rows, rows), rows)
        dst = slice(b * rows, (b + 1) * rows)
        q_s[dst, :] = proj[src, 0:width]
        k_s[dst, :] = proj[src, width : 2 * width]
        value = proj[src, 2 * width : 3 * width]
        v_s[dst, :] = value
        vt_s[:, dst] = jnp.transpose(value)
    cols = [slice(h * size, (h + 1) * size) for h in range(heads)]

    def query_block(index, _):
        here = tile_rows(index)
        queries = [q_s[here, c] for c in cols]

        def scores_of(tile, h):
            return dot_nt(k_s[tile_rows(tile), cols[h]], queries[h]) * factor

        def weigh(tile, h, scores, highest):
            weights = jnp.exp2(scores - highest)
            total = jnp.sum(weights, axis=0, keepdims=True)
            return total, dot_nn(vt_s[cols[h], tile_rows(tile)], low(weights))

        start = []
        for h in range(heads):
            scores = causal(scores_of(index, h))
            highest = jnp.max(scores, axis=0, keepdims=True)
            start.append((highest, *weigh(index, h, scores, highest)))

        def step(tile, carry):
            out = []
            for h in range(heads):
                highest, total, acc = carry[h]
                scores = scores_of(tile, h)
                higher = jnp.maximum(highest, jnp.max(scores, axis=0, keepdims=True))
                keep = jnp.exp2(highest - higher)
                more, add = weigh(tile, h, scores, higher)
                out.append((higher, total * keep + more, acc * keep + add))
            return tuple(out)

        done = lax.fori_loop(first_key_tile(index, splits), index, step, tuple(start))
        for h in range(heads):
            highest, total, acc = done[h]
            attended[here, cols[h]] = jnp.transpose(acc / total)
            lse[index, h : h + 1, :] = highest + jnp.log2(total)
        return 0

    lax.fori_loop(0, length // TILE, query_block, 0)

    total = [(memory[h], norm[h : h + 1, :]) for h in range(heads)]
    now = list(total)
    per = SHORT // TILE
    for half in range(length // SHORT):
        fresh = True if half % 2 == 0 else splits[half // 2] == 1
        both = []
        for h in range(heads):
            now[h] = tuple(jnp.where(fresh, new, old) for new, old in zip(total[h], now[h]))
            states[half, h] = now[h][0]
            norms[half, h : h + 1, :] = now[h][1]
            both.append(state_matrix(*now[h]))
        for index in range(half * per, (half + 1) * per):
            here = slice(index * TILE, (index + 1) * TILE)
            for h in range(heads):
                query_feat = feature(q_s[here, cols[h]].astype(jnp.float32))
                key_feat = feature(k_s[here, cols[h]].astype(jnp.float32))
                read = dot_nn(low(query_feat), both[h])
                recalled = read[:, :size] / read[:, size:]
                merged[here, cols[h]] = low(mix[h] * recalled + (1.0 - mix[h]) * attended[here, cols[h]])
                back = dot_nn(low(key_feat), both[h])
                miss = v_s[here, cols[h]].astype(jnp.float32) - back[:, :size] / back[:, size:]
                total[h] = (
                    total[h][0] + dot_tn(low(key_feat), low(miss)),
                    total[h][1] + jnp.sum(key_feat, axis=0, keepdims=True),
                )
    for h in range(heads):
        memory_out[h] = total[h][0]
        norm_out[h : h + 1, :] = total[h][1]


def backward_kernel(
    order, splits, mix, proj, combined_grad, attended, lse, states, norms,
    proj_grad, gate,
    q_s, k_s, v_s, kt_s, g_s, delta_s, dq_s, dk_s, dv_s, *, rows, heads, size,
):
    length = proj.shape[0]
    width = heads * size
    scale = size ** (-0.5)
    factor = scale * LOG2E
    for b in range(length // rows):
        src = pl.ds(pl.multiple_of(order[b] * rows, rows), rows)
        dst = slice(b * rows, (b + 1) * rows)
        q_s[dst, :] = proj[src, 0:width]
        key = proj[src, width : 2 * width]
        k_s[dst, :] = key
        v_s[dst, :] = proj[src, 2 * width : 3 * width]
        kt_s[:, dst] = jnp.transpose(key)
    cols = [slice(h * size, (h + 1) * size) for h in range(heads)]
    ones = jnp.ones((8, size), jnp.float32)
    slots = length // (2 * SHORT)
    per = SHORT // TILE

    for h in range(heads):
        share = mix[h]
        col = cols[h]
        gate_sum = jnp.zeros((1, size), jnp.float32)
        next_m, next_n = jnp.zeros((size, size), jnp.float32), jnp.zeros((1, size), jnp.float32)
        for slot in reversed(range(slots)):
            split = splits[slot] == 1
            later_m, later_n = None, None
            for half in (2 * slot + 1, 2 * slot):
                last = half == 2 * slots - 1
                if half % 2 == 1:
                    up_m, up_n = next_m, next_n
                else:
                    up_m = jnp.where(split, later_m, next_m)
                    up_n = jnp.where(split, later_n, next_n)
                memory = states[half, h]
                norm_row = norms[half, h : h + 1, :]
                both = state_matrix(memory, norm_row)
                low_memory = low(memory)
                low_up = low(up_m)
                up_both = jnp.concatenate([low_up, low_memory], axis=1)

                def chunk(index, carry, both=both, low_memory=low_memory, low_up=low_up, up_both=up_both, norm_row=norm_row, up_n=up_n, last=last):
                    here = slice(index * TILE, (index + 1) * TILE)
                    sum_m, sum_n, sum_gate = carry
                    att = attended[here, col]
                    grad = combined_grad[here, col].astype(jnp.float32)
                    query_feat = feature(q_s[here, col].astype(jnp.float32))
                    read = dot_nn(low(query_feat), both)
                    inverse = 1.0 / read[:, size:]
                    recalled = read[:, :size] * inverse
                    recalled_grad = share * grad
                    attended_grad = low((1.0 - share) * grad)
                    g_s[here, col] = attended_grad
                    sums = lax.dot_general(
                        ones, attended_grad.astype(jnp.float32) * att, (((1,), (1,)), ((), ())),
                        precision=lax.Precision.HIGHEST, preferred_element_type=jnp.float32,
                    )
                    delta_s[index, h : h + 1, :] = sums[0:1, :]
                    sum_gate = sum_gate + jnp.sum(grad * (recalled - att), axis=0, keepdims=True)
                    scaled = recalled_grad * inverse
                    den_grad = -jnp.sum(recalled_grad * recalled, axis=1, keepdims=True) * inverse
                    query_feat_grad = dot_nt(low(scaled), low_memory) + den_grad * norm_row
                    dq_s[here, col] = query_feat_grad * jnp.minimum(query_feat, 1.0)
                    sum_m = sum_m + dot_tn(low(query_feat), low(scaled))
                    sum_n = sum_n + jnp.sum(den_grad * query_feat, axis=0, keepdims=True)
                    if last:
                        dk_s[here, col] = jnp.zeros((TILE, size), jnp.float32)
                        dv_s[here, col] = jnp.zeros((TILE, size), jnp.float32)
                    else:
                        key_feat = feature(k_s[here, col].astype(jnp.float32))
                        back = dot_nn(low(key_feat), both)
                        key_inverse = 1.0 / back[:, size:]
                        retrieved = back[:, :size] * key_inverse
                        miss = v_s[here, col].astype(jnp.float32) - retrieved
                        miss_grad = dot_nn(low(key_feat), low_up)
                        dv_s[here, col] = miss_grad
                        pair = jnp.concatenate([low(miss), low(-miss_grad * key_inverse)], axis=1)
                        along = jnp.sum(miss_grad * retrieved, axis=1, keepdims=True) * key_inverse
                        key_feat_grad = dot_nt(pair, up_both) + along * norm_row + up_n
                        dk_s[here, col] = key_feat_grad * jnp.minimum(key_feat, 1.0)
                    return sum_m, sum_n, sum_gate

                carry = (jnp.zeros((size, size), jnp.float32), jnp.zeros((1, size), jnp.float32), gate_sum)
                for index in range(half * per, (half + 1) * per):
                    carry = chunk(index, carry)
                sum_m, sum_n, gate_sum = carry
                if half % 2 == 1:
                    later_m, later_n = sum_m, sum_n
                else:
                    next_m = jnp.where(split, sum_m, sum_m + later_m)
                    next_n = jnp.where(split, sum_n, sum_n + later_n)
        gate[h : h + 1, :] = gate_sum

    def query_block(index, _):
        here = tile_rows(index)

        def part(tile, h, mask):
            there = tile_rows(tile)
            col = cols[h]
            queries, grads, keys = q_s[here, col], g_s[here, col], k_s[there, col]
            scores = dot_nt(keys, queries) * factor
            if mask:
                scores = causal(scores)
            probs = jnp.exp2(scores - lse[index, h : h + 1, :])
            prob_grad = dot_nt(v_s[there, col], grads)
            score_grad = low(probs * (prob_grad - delta_s[index, h : h + 1, :]))
            dv_s[there, col] += dot_nn(low(probs), grads)
            dk_s[there, col] += dot_nn(score_grad, queries) * scale
            return dot_nn(kt_s[col, there], score_grad)

        start = tuple(part(index, h, True) for h in range(heads))

        def step(tile, carry):
            return tuple(carry[h] + part(tile, h, False) for h in range(heads))

        done = lax.fori_loop(first_key_tile(index, splits), index, step, start)
        for h in range(heads):
            dq_s[here, cols[h]] += jnp.transpose(done[h]) * scale
        return 0

    lax.fori_loop(0, length // TILE, query_block, 0)
    for b in range(length // rows):
        dst = pl.ds(pl.multiple_of(order[b] * rows, rows), rows)
        src = slice(b * rows, (b + 1) * rows)
        proj_grad[dst, 0:width] = low(dq_s[src, :])
        proj_grad[dst, width : 2 * width] = low(dk_s[src, :])
        proj_grad[dst, 2 * width : 3 * width] = low(dv_s[src, :])


SMEM = pl.BlockSpec(memory_space=pltpu.SMEM)
VMEM = pl.BlockSpec(memory_space=pltpu.VMEM)


def attend_forward(order, splits, mix, proj, memory, norm, rows):
    heads, size, _ = memory.shape
    length, width = proj.shape[0], heads * size
    halves, tiles = length // SHORT, length // TILE
    shapes = [
        jax.ShapeDtypeStruct((length, width), jnp.bfloat16),
        jax.ShapeDtypeStruct((length, width), jnp.float32),
        jax.ShapeDtypeStruct((tiles, heads, TILE), jnp.float32),
        jax.ShapeDtypeStruct((halves, heads, size, size), jnp.float32),
        jax.ShapeDtypeStruct((halves, heads, size), jnp.float32),
        jax.ShapeDtypeStruct((heads, size, size), jnp.float32),
        jax.ShapeDtypeStruct((heads, size), jnp.float32),
    ]
    whole = pltpu.VMEM((length, width), jnp.bfloat16)
    return pl.pallas_call(
        functools.partial(forward_kernel, rows=rows, heads=heads, size=size),
        out_shape=shapes,
        in_specs=[SMEM] * 3 + [VMEM] * 3,
        out_specs=[VMEM] * len(shapes),
        scratch_shapes=[whole, whole, whole, pltpu.VMEM((width, length), jnp.bfloat16)],
        compiler_params=pltpu.CompilerParams(vmem_limit_bytes=VMEM_LIMIT),
        cost_estimate=NO_COST,
    )(order, splits, mix, proj, memory, norm)


def attend_backward(order, splits, mix, proj, combined_grad, attended, lse, states, norms, rows):
    _, heads, size, _ = states.shape
    length, width = proj.shape[0], heads * size
    tiles = length // TILE
    shapes = [
        jax.ShapeDtypeStruct((length, 3 * width), jnp.bfloat16),
        jax.ShapeDtypeStruct((heads, size), jnp.float32),
    ]
    whole = pltpu.VMEM((length, width), jnp.bfloat16)
    wide = pltpu.VMEM((length, width), jnp.float32)
    return pl.pallas_call(
        functools.partial(backward_kernel, rows=rows, heads=heads, size=size),
        out_shape=shapes,
        in_specs=[SMEM] * 3 + [VMEM] * 6,
        out_specs=[VMEM] * len(shapes),
        scratch_shapes=[
            whole, whole, whole, pltpu.VMEM((width, length), jnp.bfloat16), whole,
            pltpu.VMEM((tiles, heads, TILE), jnp.float32), wide, wide, wide,
        ],
        compiler_params=pltpu.CompilerParams(vmem_limit_bytes=VMEM_LIMIT),
        cost_estimate=NO_COST,
    )(order, splits, mix, proj, combined_grad, attended, lse, states, norms)


def fill(whole, pieces):
    rows = pieces[0].shape[0]
    for place, piece in enumerate(pieces):
        whole[place * rows : (place + 1) * rows, :] = piece[...]


def project_kernel(*refs, count):
    pieces, weight = refs[:count], refs[count]
    normed_all, proj_all = refs[-2:]
    width = normed_all.shape[1]

    @pl.when(pl.program_id(0) == 0)
    def _():
        begin = 0
        for piece in pieces:
            here = slice(begin, begin + piece.shape[0])
            normed_all[here, :] = piece[:, :width]
            begin += piece.shape[0]

    proj_all[...] = low(dot_nn(normed_all[...], weight[...]))


def widen_kernel(*refs, moves):
    out, parts = refs[-1], refs[:-1]
    for part, begin, size, place, column in moves:
        out[:, place, column : column + size] = parts[part][:, begin : begin + size].astype(jnp.float32)


def widen(parts, moves, shape):
    rows = shape[0]
    tall = min(rows, 128)
    return pl.pallas_call(
        functools.partial(widen_kernel, moves=moves),
        grid=(rows // tall,),
        out_shape=jax.ShapeDtypeStruct(shape, jnp.float32),
        in_specs=[pl.BlockSpec((tall, part.shape[1]), lambda i: (i, 0)) for part in parts],
        out_specs=pl.BlockSpec((tall, *shape[1:]), lambda i: (i, 0, 0)),
        cost_estimate=NO_COST,
    )(*parts)


def feed_kernel(*refs, count):
    normed, cots = refs[:count], refs[count : 2 * count]
    w_both, w_down = refs[2 * count : 2 * count + 2]
    result_s, grad_s = refs[-2:]
    results, grads = refs[-2 - 2 * count : -2 - count], refs[-2 - count : -2]
    normed_all, cot_all, hidden, first_grad, second_grad = refs[-7 - 2 * count : -2 - 2 * count]
    step = pl.program_id(0)
    half = pl.num_programs(0) // 2
    tile = w_down.shape[0]

    @pl.when(step == 0)
    def _():
        fill(normed_all, normed)
        fill(cot_all, cots)

    gate_up = dot_nn(normed_all[...], w_both[...])
    hidden_grad = dot_nt(cot_all[...], w_down[...])
    gate, up = gate_up[:, :tile], gate_up[:, tile:]
    sigmoid_gate = 1.0 / (1.0 + jnp.exp(-gate))
    activated = gate * sigmoid_gate
    low_hidden = low(activated * up)
    low_gate = low(hidden_grad * up * (sigmoid_gate + activated * (1.0 - sigmoid_gate)))
    low_up = low(hidden_grad * activated)
    hidden[...] = low_hidden
    both_grad = jnp.concatenate([low_gate, low_up], axis=1)

    @pl.when(step < half)
    def _():
        first_grad[...] = both_grad

    @pl.when(step >= half)
    def _():
        second_grad[...] = both_grad

    @pl.when(step == 0)
    def _():
        result_s[...] = dot_nn(low_hidden, w_down[...])
        grad_s[...] = dot_nt(both_grad, w_both[...])

    @pl.when(step > 0)
    def _():
        result_s[...] += dot_nn(low_hidden, w_down[...])
        grad_s[...] += dot_nt(both_grad, w_both[...])

    @pl.when(step == pl.num_programs(0) - 1)
    def _():
        rows = results[0].shape[0]
        for place in range(count):
            here = slice(place * rows, (place + 1) * rows)
            results[place][...] = low(result_s[here, :])
            grads[place][...] = low(grad_s[here, :])


NO_COST = pl.CostEstimate(flops=4_000_000_000, bytes_accessed=4096, transcendentals=0)
ANY = pl.BlockSpec(memory_space=pl.ANY)


def project_blocks(pieces, weight, place, length, before):
    width, wide = weight.shape
    count = len(pieces)
    tall = sum(piece.shape[0] for piece in pieces)
    tile = 256 if wide % 256 == 0 else 128
    return pl.pallas_call(
        functools.partial(project_kernel, count=count),
        grid=(wide // tile,),
        out_shape=[
            jax.ShapeDtypeStruct((length, width), jnp.bfloat16),
            jax.ShapeDtypeStruct((length, wide), jnp.bfloat16),
        ],
        in_specs=[pl.BlockSpec(piece.shape, lambda j: (0, 0)) for piece in pieces]
        + [pl.BlockSpec((width, tile), lambda j: (0, j))]
        + [ANY] * len(before),
        out_specs=[
            pl.BlockSpec((tall, width), lambda j: (place, 0)),
            pl.BlockSpec((tall, tile), lambda j: (place, j)),
        ],
        input_output_aliases={count + 1 + i: i for i in range(len(before))},
        compiler_params=pltpu.CompilerParams(vmem_limit_bytes=VMEM_LIMIT),
        cost_estimate=NO_COST,
    )(*pieces, weight, *before)


def feed_blocks(normed, cots, f_in, f_out, place, length, before):
    count = len(normed)
    rows, width = normed[0].shape
    tall, wide = count * rows, f_out.shape[0]
    tile = min(FEED_TILE, wide)
    tiles = wide // tile
    piece = pl.BlockSpec((rows, width), lambda j: (0, 0))
    kept = pl.BlockSpec((tall, width), lambda j: (place, 0))
    part = pl.BlockSpec((tall, tile), lambda j: (place, j))
    first = pl.BlockSpec((tall, 2 * tile), lambda j: (place, jnp.minimum(j, tiles // 2 - 1)))
    second = pl.BlockSpec((tall, 2 * tile), lambda j: (place, jnp.maximum(j - tiles // 2, 0)))
    outs = pl.pallas_call(
        functools.partial(feed_kernel, count=count),
        grid=(tiles,),
        out_shape=[jax.ShapeDtypeStruct((length, width), jnp.bfloat16)] * 2
        + [jax.ShapeDtypeStruct((length, wide), jnp.bfloat16)] * 3
        + [jax.ShapeDtypeStruct((rows, width), jnp.bfloat16)] * (2 * count),
        in_specs=[piece] * (2 * count)
        + [
            pl.BlockSpec((width, 2 * tile), lambda j: (0, j)),
            pl.BlockSpec((tile, width), lambda j: (j, 0)),
        ]
        + [ANY] * len(before),
        out_specs=[kept] * 2 + [part, first, second] + [piece] * (2 * count),
        scratch_shapes=[pltpu.VMEM((tall, width), jnp.float32)] * 2,
        input_output_aliases={2 * count + 2 + i: i for i in range(len(before))},
        compiler_params=pltpu.CompilerParams(vmem_limit_bytes=VMEM_LIMIT),
        cost_estimate=NO_COST,
    )(*normed, *cots, f_in, f_out, *before)
    return outs[:5], outs[5 : 5 + count], outs[5 + count :]


def ring_of(count):
    deep = 4 if count % 4 == 0 else count
    across = count // deep
    ring = [z * across for z in range(deep)]
    for z in reversed(range(deep)):
        turn = range(1, across)
        ring += [z * across + y for y in (turn if (deep - 1 - z) % 2 == 0 else reversed(turn))]
    return ring


class Ring:
    def __init__(self, count):
        self.count = count
        ring = ring_of(count)
        self.ahead = [(ring[p], ring[(p + 1) % count]) for p in range(count)]
        self.behind = [(b, a) for a, b in self.ahead]
        places = [0] * count
        for place, index in enumerate(ring):
            places[index] = place
        places = jnp.array(places, jnp.int32)
        self.slots = [0] * count
        self.slots[count // 2] = 1
        for step in range(1, count // 2):
            self.slots[count - step], self.slots[step] = 2 * step, 2 * step + 1
        here = places[lax.axis_index("blk")]
        self.order = jnp.array(self.slots, jnp.int32)[lax.rem(places - here + count, count)]
        around = lax.rem(jnp.arange(count, dtype=jnp.int32) + here, count)
        self.ahead_index = jnp.array(ring, jnp.int32)[around]

    def forth(self, values):
        return lax.ppermute(values, "blk", self.ahead)

    def back(self, values):
        return lax.ppermute(values, "blk", self.behind)


class Gather:
    def __init__(self, ring, block):
        self.ring = ring
        self.groups = [(block,)]

    def hop(self, *earlier):
        ring, half = self.ring, self.ring.count // 2
        last = self.groups[-1]
        behind, ahead = after((last[0], last[-1]), *earlier)
        if len(self.groups) == half:
            middle = behind.shape[0] // 2
            behind, ahead = behind[:middle], ahead[middle:]
        self.groups.append((ring.forth(behind), ring.back(ahead)))
        return self.groups[-1]

    def place(self, step):
        return {0: 0, self.ring.count // 2: 1}.get(step, step)


class Scatter:
    def __init__(self, ring, partial, axis=0):
        self.ring = ring
        self.partial = partial
        self.axis = axis
        self.step = ring.count // 2
        self.sent = self.moved = self.rider = self.parts = None
        self.begin = 0
        self.fresh = True

    def messages(self, *earlier):
        half, step = self.ring.count // 2, self.step
        self.step -= 1
        if step == half:
            return after(tuple(self.partial(half)), *earlier)
        forward, backward = self.came(*earlier)
        if step == half - 1:
            extra = forward.shape[self.axis]
            forward = jnp.pad(forward, [(0, extra if axis == self.axis else 0) for axis in (0, 1)])
            backward = jnp.pad(backward, [(extra if axis == self.axis else 0, 0) for axis in (0, 1)])
        parts = self.parts or (self.partial(step), self.partial(self.ring.count - step))
        self.parts = None
        forward, backward = parts[0].astype(jnp.float32) + forward, parts[1].astype(jnp.float32) + backward
        return low(forward), low(backward)

    def compute(self, *earlier):
        self.parts = after((low(self.partial(self.step)), low(self.partial(self.ring.count - self.step))), *earlier)

    def came(self, *earlier):
        width = self.partial(0).shape[1]
        return [
            part[:, self.begin : self.begin + width].astype(jnp.float32) for part in after(self.moved, *earlier)
        ]

    def prepare(self, *earlier, rider=None):
        self.sent = self.messages(*earlier)
        self.fresh = False
        self.rider = rider
        if rider is not None:
            self.sent = tuple(
                jnp.concatenate(pair, axis=1) for pair in zip(self.sent, rider.messages(*earlier))
            )
        self.sent = after(self.sent)

    def hop(self, *earlier):
        if self.fresh:
            self.prepare()
        self.fresh = True
        forward, backward = self.sent = after(self.sent, *earlier)
        self.moved = (self.ring.forth(forward), self.ring.back(backward))

    def hold(self, *others):
        self.moved = after(self.moved, *others)
        if self.rider is not None:
            self.rider.moved, self.rider.begin = self.moved, self.partial(0).shape[1]
            self.rider = None

    def total(self):
        forward, backward = self.came()
        return self.partial(0).astype(jnp.float32) + forward + backward


def after(values, *earlier):
    return lax.optimization_barrier((values, earlier))[0]


def sum_axis(values, axis):
    size = lax.axis_size(axis)
    terms = [values] + [
        lax.ppermute(values, axis, [(i, i ^ step) for i in range(size)]) for step in range(1, size)
    ]
    while len(terms) > 1:
        terms = [left + right for left, right in zip(terms[::2], terms[1::2])]
    return terms[0]


def swap_sum(values, axis, step, *earlier):
    size = lax.axis_size(axis)
    return values + after(lax.ppermute(values, axis, [(i, i ^ step) for i in range(size)]), *earlier)


def halve_rows(values, bit):
    size = lax.axis_size("seq")
    mine = lax.div(lax.axis_index("seq"), bit) % 2
    left = size // (2 * bit)
    blocks = values.reshape(left, 2, values.shape[0] // (2 * left), values.shape[1])
    kept = lax.dynamic_index_in_dim(blocks, mine, 1, keepdims=False)
    sent = lax.dynamic_index_in_dim(blocks, 1 - mine, 1, keepdims=False)
    moved = lax.ppermute(sent, "seq", [(i, i ^ bit) for i in range(size)])
    return low(kept.astype(jnp.float32) + moved.astype(jnp.float32)).reshape(-1, values.shape[1])


def rms_parts(values):
    scale_rows = lax.rsqrt(jnp.mean(values * values, axis=-1, keepdims=True) + EPSILON)
    return (scale_rows, values * scale_rows)


def rms_back(unit_grad, unit, scale_rows):
    return scale_rows * (unit_grad - unit * jnp.mean(unit_grad * unit, axis=-1, keepdims=True))


def sum_over_seq(values, dimension):
    return lax.psum_scatter(low(values), "seq", scatter_dimension=dimension, tiled=True)


def per_device(
    tokens,
    cotangent,
    grouping,
    memory_start,
    normalizer_start,
    gain_attention,
    attention_in,
    gate_logit,
    attention_out,
    gain_feed,
    feed_in,
    feed_out,
):
    rows, width = tokens.shape
    heads_here = memory_start.shape[1]
    count = lax.axis_size("blk")
    ring = Ring(count)
    splits = grouping[0]
    head_first = lax.axis_index("blk") * heads_here
    mix = jax.nn.sigmoid(lax.dynamic_slice_in_dim(gate_logit, head_first, heads_here, 0))

    def whole(weight, axis):
        return lax.all_gather(weight, "seq", axis=axis, tiled=True)

    half = count // 2
    tokens_full = tokens.astype(jnp.float32)
    scale_first, unit_first = rms_parts(tokens_full)

    length = rows * count
    w_in = whole(attention_in.reshape(attention_in.shape[0], -1), 0)
    gather_a = Gather(
        ring, jnp.concatenate([low(unit_first * gain_attention), attention_out.reshape(rows, -1)], axis=1)
    )

    gather_a.hop()
    feed_tile = min(FEED_TILE, feed_in.shape[2])
    feed_tiles = feed_in.shape[2] // feed_tile
    f_in = after(feed_in, gather_a.groups[0]).reshape(-1, 2, feed_tiles, feed_tile)
    f_in = f_in.transpose(0, 2, 1, 3).reshape(feed_in.shape[0], -1)
    f_in = whole(after(f_in, w_in, gather_a.groups[1]), 0)
    kept = []
    for step in range(2, half + 1):
        gather_a.hop(*kept[1:2])
        if step > 2:
            kept = project_blocks(gather_a.groups[step - 2], w_in, step - 2, length, kept)
    kept = project_blocks(gather_a.groups[half - 1], w_in, half - 1, length, kept)
    gather_a.groups[half] = after(gather_a.groups[half], kept[1])
    normed_a, proj = project_blocks(gather_a.groups[0] + gather_a.groups[half], w_in, 0, length, kept)
    w_out = jnp.zeros((length, gather_a.groups[0][0].shape[1] - width), jnp.bfloat16)
    for step, group in enumerate(gather_a.groups):
        for piece, d, begin in zip(group, (-step % count, step), (0, rows // 2 if step == half else 0)):
            start = ring.ahead_index[d] * rows + begin
            w_out = lax.dynamic_update_slice_in_dim(w_out, piece[:, width:], start, 0)
    w_out = whole(after(w_out.reshape(-1, attention_out.shape[1]), f_in), 1)

    gather_c = Gather(ring, after(cotangent, gather_a.groups[half]))
    gather_c.hop()
    merged, attended, lse, states, norms, memory_final, norm_final = attend_forward(
        ring.order, splits, mix, proj, memory_start[0], normalizer_start[0], rows
    )
    merged_mine = lax.all_to_all(after(merged, gather_c.groups[1]), "blk", 0, 1, tiled=True)
    f_out = whole(after(feed_out, w_out, merged_mine), 1)
    while len(gather_c.groups) < half - 1:
        gather_c.hop(merged_mine)
    middle = tokens_full + dot_nn(merged_mine, w_out)
    scale_second, unit_second = rms_parts(middle)
    gather_f = Gather(ring, after(low(unit_second * gain_feed), gather_c.groups[-1]))
    result_part, normed_f_part = {}, {}
    kept = []

    def feed(step, kept):
        kept, results, grads = feed_blocks(
            gather_f.groups[step], gather_c.groups[step], f_in, f_out, gather_f.place(step), length, kept
        )
        if step == half:
            result_part[half], normed_f_part[half] = results, grads
        else:
            for d, result, grad in zip((-step % count, step), results, grads):
                result_part[d], normed_f_part[d] = result, grad
        return kept

    for step in range(1, half + 1):
        gather_f.hop(gather_c.groups[-1], *kept[2:3])
        if step > 1:
            kept = feed(step - 1 if step < half else half, kept)
        if len(gather_c.groups) <= half:
            gather_c.hop(gather_f.groups[step], *(kept[2:3] if step > 1 else []))
        if step == 1:
            kept = feed(0, kept)
    kept = feed(half - 1, kept)
    normed_f, cot, hidden, first_grad, second_grad = kept

    scatter_f = Scatter(ring, lambda d: normed_f_part[d])
    scatter_r = Scatter(ring, lambda d: result_part[d])
    scatter_f.hop()
    scatter_r.hop(scatter_f.sent)
    scatter_f.hop(scatter_r.moved)
    for _ in range(half - 4):
        scatter_f.hop()
    feed_out_local = low(dot_tn(hidden, after(cot, scatter_f.sent)))
    scatter_f.hold(feed_out_local)
    feed_out_grad = sum_over_seq(after(feed_out_local, scatter_f.moved), 1)
    scatter_f.hop()
    feed_first_local = low(dot_tn(normed_f, after(first_grad, scatter_f.sent)))
    scatter_f.hold(feed_first_local)
    scatter_f.hop()
    feed_second_local = low(dot_tn(normed_f, after(second_grad, scatter_f.sent)))
    scatter_f.hold(feed_second_local)
    normed_f_grad = scatter_f.total()
    feed_first_grad = sum_over_seq(after(feed_first_local, feed_out_grad, normed_f_grad), 0)
    scatter_r.prepare()
    gain_feed_part = jnp.sum(normed_f_grad * unit_second, axis=0)
    middle_grad = cotangent.astype(jnp.float32) + rms_back(
        normed_f_grad * gain_feed, unit_second, scale_second
    )
    out_grad = low(middle_grad)
    combined_grad = low(dot_nt(out_grad, w_out))
    attention_out_local = low(dot_tn(merged_mine, after(out_grad, feed_second_local)))
    combined_grad = lax.all_to_all(combined_grad, "blk", 1, 0, tiled=True)
    combined_grad = after(combined_grad, attention_out_local, scatter_r.sent)
    out_sum = sum_over_seq(after(attention_out_local, feed_first_grad, combined_grad), 1)
    scatter_r.hop(combined_grad)
    proj_grad, gate_rows = attend_backward(
        ring.order, splits, mix, proj, combined_grad,
        attended, lse, states, norms, rows,
    )
    def in_two(values):
        return values[: values.shape[0] // 2], values[values.shape[0] // 2 :]

    def normed_a_part(d):
        first = ring.slots[d] * rows
        if d == half:
            return [low(dot_nt(part, w_in)) for part in in_two(proj_grad[first : first + rows])]
        return dot_nt(proj_grad[first : first + rows], w_in)

    proj_grad = after(proj_grad, scatter_r.moved)
    def attention_out_part(d):
        high = attention_out.shape[0]
        part = lax.dynamic_slice_in_dim(out_sum, ring.ahead_index[d] * high, high, 0).reshape(rows, -1)
        return (part[:, : part.shape[1] // 2], part[:, part.shape[1] // 2 :]) if d == half else part

    scatter_o = Scatter(ring, attention_out_part, axis=1)

    def rider():
        return scatter_o if scatter_o.step > 0 else None

    scatter_a = Scatter(ring, normed_a_part)
    scatter_a.hop()
    scatter_a.compute(scatter_a.sent)
    scatter_a.hold(scatter_a.parts)
    scatter_a.hop()
    scatter_r.prepare(scatter_a.sent, rider=rider())
    scatter_a.hold(scatter_r.sent)
    scatter_r.hop(scatter_a.moved)
    attention_in_local = low(dot_tn(normed_a, after(proj_grad, scatter_a.moved)))
    feed_second_grad = sum_over_seq(after(feed_second_local, out_sum, scatter_a.moved), 0)
    gain_attention_part = jnp.sum(attention_in_local.astype(jnp.float32) * w_in.astype(jnp.float32), axis=1) / gain_attention
    gate_part = jnp.sum(gate_rows, axis=1) * mix * (1.0 - mix)
    gate_full = lax.dynamic_update_slice_in_dim(
        jnp.zeros(gate_logit.shape, jnp.float32), gate_part, head_first, 0
    )
    sums = jnp.concatenate([gain_attention_part, gain_feed_part, gate_full])
    scatter_a.compute(scatter_a.moved)
    sums = sum_axis(sums, "seq")
    scatter_r.hold(scatter_a.parts, attention_in_local, sums)
    swaps = [1 << bit for bit in range(count.bit_length() - 1)]
    halvings = [1 << bit for bit in reversed(range(lax.axis_size("seq").bit_length() - 1))]
    attention_in_grad = attention_in_local
    while scatter_a.step > 1:
        scatter_a.prepare(rider=rider())
        scatter_a.hop(scatter_r.moved)
        if swaps:
            sums = swap_sum(after(sums, scatter_a.sent), "blk", swaps.pop())
        if halvings:
            attention_in_grad = halve_rows(after(attention_in_grad, scatter_a.sent), halvings.pop())
        scatter_a.hold(sums, attention_in_grad)
        scatter_r.prepare(rider=rider())
        scatter_r.hop(scatter_a.moved)
        scatter_a.compute(scatter_r.sent)
        if swaps:
            sums = swap_sum(after(sums, scatter_r.sent), "blk", swaps.pop())
        if halvings:
            attention_in_grad = halve_rows(after(attention_in_grad, scatter_r.sent), halvings.pop())
        scatter_r.hold(scatter_a.parts, sums, attention_in_grad)
    scatter_a.prepare(rider=rider())
    scatter_a.hop()
    sums = after(sums, scatter_a.sent)
    while len(swaps) > 1:
        sums = swap_sum(sums, "blk", swaps.pop())
    while halvings:
        attention_in_grad = halve_rows(after(attention_in_grad, scatter_a.sent), halvings.pop())
    halves = after((feed_first_grad, feed_second_grad), scatter_a.sent)
    moves = []
    for tile in range(feed_tiles):
        part, begin = divmod(2 * feed_tile * tile, feed_in.shape[2])
        for place in range(2):
            moves.append((part, begin + place * feed_tile, feed_tile, place, tile * feed_tile))
    feed_in_grad = widen(halves, moves, feed_in.shape)
    size = attention_in.shape[2]
    moves = [(0, place * size, size, place, 0) for place in range(attention_in.shape[1])]
    attention_in_grad = widen((after(attention_in_grad, scatter_a.sent),), moves, attention_in.shape)
    result, feed_out_grad = after((low(middle + scatter_r.total()), feed_out_grad), scatter_a.sent)
    feed_out_grad = feed_out_grad.astype(jnp.float32)
    while swaps:
        sums = swap_sum(sums, "blk", swaps.pop(), result, feed_in_grad, feed_out_grad, attention_in_grad)
    scatter_a.hold(sums)
    attention_out_grad = scatter_o.total().reshape(attention_out.shape)
    normed_a_grad = scatter_a.total()
    token_grad = middle_grad + rms_back(normed_a_grad * gain_attention, unit_first, scale_first)
    return (
        result,
        token_grad,
        sums[:width],
        attention_in_grad,
        sums[2 * width :],
        attention_out_grad.astype(jnp.float32),
        sums[width : 2 * width],
        feed_in_grad,
        feed_out_grad,
        memory_final[None],
        norm_final[None],
    )


def solution(mesh):
    in_specs = (
        P(("seq", "blk"), None),
        P(("seq", "blk"), None),
        P("seq", None),
        P("seq", "blk", None, None),
        P("seq", "blk", None),
        P(),
        P("seq", None, "blk"),
        P(),
        P("blk", "seq"),
        P(),
        P("seq", None, "blk"),
        P("blk", "seq"),
    )
    out_specs = (
        P(("seq", "blk"), None),
        P(("seq", "blk"), None),
        P(),
        P("seq", None, "blk"),
        P(),
        P("blk", "seq"),
        P(),
        P("seq", None, "blk"),
        P("blk", "seq"),
        P("seq", "blk", None, None),
        P("seq", "blk", None),
    )
    return jax.shard_map(
        per_device, mesh=mesh, in_specs=in_specs, out_specs=out_specs, check_vma=False
    )
```

```python
import functools
import math

import jax
import jax.numpy as jnp
from jax import lax
from jax.experimental import pallas as pl
from jax.experimental.pallas import tpu as pltpu
from jax.sharding import PartitionSpec as P

SHORT = 1024
TILE = 512
FEED_TILE = 256
EPSILON = 1e-06
MASKED = -1e30
LOG2E = math.log2(math.e)
VMEM_LIMIT = 60 * 1024 * 1024


def dot_nn(left, right):
    return lax.dot_general(left, right, (((1,), (0,)), ((), ())), preferred_element_type=jnp.float32)


def dot_nt(left, right):
    return lax.dot_general(left, right, (((1,), (1,)), ((), ())), preferred_element_type=jnp.float32)


def dot_tn(left, right):
    return lax.dot_general(left, right, (((0,), (0,)), ((), ())), preferred_element_type=jnp.float32)


def low(values):
    return values.astype(jnp.bfloat16)


def feature(values):
    return jnp.where(values > 0, values + 1.0, jnp.exp(jnp.minimum(values, 0.0)))


def first_key_tile(index, splits):
    per = 2 * SHORT // TILE
    slot = lax.div(index, per)
    second = (lax.rem(index, per) >= per // 2) & (splits[slot] == 1)
    return slot * per + jnp.where(second, per // 2, 0)


def tile_rows(index):
    return pl.ds(pl.multiple_of(index * TILE, TILE), TILE)


def causal(scores):
    key_pos = lax.broadcasted_iota(jnp.int32, scores.shape, 0)
    query_pos = lax.broadcasted_iota(jnp.int32, scores.shape, 1)
    return jnp.where(key_pos <= query_pos, scores, MASKED)


def state_matrix(memory, norm_row):
    spread = jnp.transpose(jnp.broadcast_to(norm_row, memory.shape))
    return low(jnp.concatenate([memory, spread], axis=1))


def forward_kernel(
    order, splits, mix, proj, memory, norm,
    merged, attended, lse, states, norms, memory_out, norm_out,
    q_s, k_s, v_s, vt_s, *, rows, heads, size,
):
    length = proj.shape[0]
    width = heads * size
    factor = size ** (-0.5) * LOG2E
    for b in range(length // rows):
        src = pl.ds(pl.multiple_of(order[b] * rows, rows), rows)
        dst = slice(b * rows, (b + 1) * rows)
        q_s[dst, :] = proj[src, 0:width]
        k_s[dst, :] = proj[src, width : 2 * width]
        value = proj[src, 2 * width : 3 * width]
        v_s[dst, :] = value
        vt_s[:, dst] = jnp.transpose(value)
    cols = [slice(h * size, (h + 1) * size) for h in range(heads)]

    def query_block(index, _):
        here = tile_rows(index)
        queries = [q_s[here, c] for c in cols]

        def scores_of(tile, h):
            return dot_nt(k_s[tile_rows(tile), cols[h]], queries[h]) * factor

        def weigh(tile, h, scores, highest):
            weights = jnp.exp2(scores - highest)
            total = jnp.sum(weights, axis=0, keepdims=True)
            return total, dot_nn(vt_s[cols[h], tile_rows(tile)], low(weights))

        start = []
        for h in range(heads):
            scores = causal(scores_of(index, h))
            highest = jnp.max(scores, axis=0, keepdims=True)
            start.append((highest, *weigh(index, h, scores, highest)))

        def step(tile, carry):
            out = []
            for h in range(heads):
                highest, total, acc = carry[h]
                scores = scores_of(tile, h)
                higher = jnp.maximum(highest, jnp.max(scores, axis=0, keepdims=True))
                keep = jnp.exp2(highest - higher)
                more, add = weigh(tile, h, scores, higher)
                out.append((higher, total * keep + more, acc * keep + add))
            return tuple(out)

        done = lax.fori_loop(first_key_tile(index, splits), index, step, tuple(start))
        for h in range(heads):
            highest, total, acc = done[h]
            attended[here, cols[h]] = jnp.transpose(acc / total)
            lse[index, h : h + 1, :] = highest + jnp.log2(total)
        return 0

    lax.fori_loop(0, length // TILE, query_block, 0)

    total = [(memory[h], norm[h : h + 1, :]) for h in range(heads)]
    now = list(total)
    per = SHORT // TILE
    for half in range(length // SHORT):
        fresh = True if half % 2 == 0 else splits[half // 2] == 1
        both = []
        for h in range(heads):
            now[h] = tuple(jnp.where(fresh, new, old) for new, old in zip(total[h], now[h]))
            states[half, h] = now[h][0]
            norms[half, h : h + 1, :] = now[h][1]
            both.append(state_matrix(*now[h]))
        for index in range(half * per, (half + 1) * per):
            here = slice(index * TILE, (index + 1) * TILE)
            for h in range(heads):
                query_feat = feature(q_s[here, cols[h]].astype(jnp.float32))
                key_feat = feature(k_s[here, cols[h]].astype(jnp.float32))
                read = dot_nn(low(query_feat), both[h])
                recalled = read[:, :size] / read[:, size:]
                merged[here, cols[h]] = low(mix[h] * recalled + (1.0 - mix[h]) * attended[here, cols[h]])
                back = dot_nn(low(key_feat), both[h])
                miss = v_s[here, cols[h]].astype(jnp.float32) - back[:, :size] / back[:, size:]
                total[h] = (
                    total[h][0] + dot_tn(low(key_feat), low(miss)),
                    total[h][1] + jnp.sum(key_feat, axis=0, keepdims=True),
                )
    for h in range(heads):
        memory_out[h] = total[h][0]
        norm_out[h : h + 1, :] = total[h][1]


def backward_kernel(
    order, splits, mix, proj, combined_grad, attended, lse, states, norms,
    proj_grad, gate,
    q_s, k_s, v_s, kt_s, g_s, delta_s, dq_s, dk_s, dv_s, *, rows, heads, size,
):
    length = proj.shape[0]
    width = heads * size
    scale = size ** (-0.5)
    factor = scale * LOG2E
    for b in range(length // rows):
        src = pl.ds(pl.multiple_of(order[b] * rows, rows), rows)
        dst = slice(b * rows, (b + 1) * rows)
        q_s[dst, :] = proj[src, 0:width]
        key = proj[src, width : 2 * width]
        k_s[dst, :] = key
        v_s[dst, :] = proj[src, 2 * width : 3 * width]
        kt_s[:, dst] = jnp.transpose(key)
    cols = [slice(h * size, (h + 1) * size) for h in range(heads)]
    ones = jnp.ones((8, size), jnp.float32)
    slots = length // (2 * SHORT)
    per = SHORT // TILE

    for h in range(heads):
        share = mix[h]
        col = cols[h]
        gate_sum = jnp.zeros((1, size), jnp.float32)
        next_m, next_n = jnp.zeros((size, size), jnp.float32), jnp.zeros((1, size), jnp.float32)
        for slot in reversed(range(slots)):
            split = splits[slot] == 1
            later_m, later_n = None, None
            for half in (2 * slot + 1, 2 * slot):
                last = half == 2 * slots - 1
                if half % 2 == 1:
                    up_m, up_n = next_m, next_n
                else:
                    up_m = jnp.where(split, later_m, next_m)
                    up_n = jnp.where(split, later_n, next_n)
                memory = states[half, h]
                norm_row = norms[half, h : h + 1, :]
                both = state_matrix(memory, norm_row)
                low_memory = low(memory)
                low_up = low(up_m)
                up_both = jnp.concatenate([low_up, low_memory], axis=1)

                def chunk(index, carry, both=both, low_memory=low_memory, low_up=low_up, up_both=up_both, norm_row=norm_row, up_n=up_n, last=last):
                    here = slice(index * TILE, (index + 1) * TILE)
                    sum_m, sum_n, sum_gate = carry
                    att = attended[here, col]
                    grad = combined_grad[here, col].astype(jnp.float32)
                    query_feat = feature(q_s[here, col].astype(jnp.float32))
                    read = dot_nn(low(query_feat), both)
                    inverse = 1.0 / read[:, size:]
                    recalled = read[:, :size] * inverse
                    recalled_grad = share * grad
                    attended_grad = low((1.0 - share) * grad)
                    g_s[here, col] = attended_grad
                    sums = lax.dot_general(
                        ones, attended_grad.astype(jnp.float32) * att, (((1,), (1,)), ((), ())),
                        precision=lax.Precision.HIGHEST, preferred_element_type=jnp.float32,
                    )
                    delta_s[index, h : h + 1, :] = sums[0:1, :]
                    sum_gate = sum_gate + jnp.sum(grad * (recalled - att), axis=0, keepdims=True)
                    scaled = recalled_grad * inverse
                    den_grad = -jnp.sum(recalled_grad * recalled, axis=1, keepdims=True) * inverse
                    query_feat_grad = dot_nt(low(scaled), low_memory) + den_grad * norm_row
                    dq_s[here, col] = query_feat_grad * jnp.minimum(query_feat, 1.0)
                    sum_m = sum_m + dot_tn(low(query_feat), low(scaled))
                    sum_n = sum_n + jnp.sum(den_grad * query_feat, axis=0, keepdims=True)
                    if last:
                        dk_s[here, col] = jnp.zeros((TILE, size), jnp.float32)
                        dv_s[here, col] = jnp.zeros((TILE, size), jnp.float32)
                    else:
                        key_feat = feature(k_s[here, col].astype(jnp.float32))
                        back = dot_nn(low(key_feat), both)
                        key_inverse = 1.0 / back[:, size:]
                        retrieved = back[:, :size] * key_inverse
                        miss = v_s[here, col].astype(jnp.float32) - retrieved
                        miss_grad = dot_nn(low(key_feat), low_up)
                        dv_s[here, col] = miss_grad
                        pair = jnp.concatenate([low(miss), low(-miss_grad * key_inverse)], axis=1)
                        along = jnp.sum(miss_grad * retrieved, axis=1, keepdims=True) * key_inverse
                        key_feat_grad = dot_nt(pair, up_both) + along * norm_row + up_n
                        dk_s[here, col] = key_feat_grad * jnp.minimum(key_feat, 1.0)
                    return sum_m, sum_n, sum_gate

                carry = (jnp.zeros((size, size), jnp.float32), jnp.zeros((1, size), jnp.float32), gate_sum)
                for index in range(half * per, (half + 1) * per):
                    carry = chunk(index, carry)
                sum_m, sum_n, gate_sum = carry
                if half % 2 == 1:
                    later_m, later_n = sum_m, sum_n
                else:
                    next_m = jnp.where(split, sum_m, sum_m + later_m)
                    next_n = jnp.where(split, sum_n, sum_n + later_n)
        gate[h : h + 1, :] = gate_sum

    def query_block(index, _):
        here = tile_rows(index)

        def part(tile, h, mask):
            there = tile_rows(tile)
            col = cols[h]
            queries, grads, keys = q_s[here, col], g_s[here, col], k_s[there, col]
            scores = dot_nt(keys, queries) * factor
            if mask:
                scores = causal(scores)
            probs = jnp.exp2(scores - lse[index, h : h + 1, :])
            prob_grad = dot_nt(v_s[there, col], grads)
            score_grad = low(probs * (prob_grad - delta_s[index, h : h + 1, :]))
            dv_s[there, col] += dot_nn(low(probs), grads)
            dk_s[there, col] += dot_nn(score_grad, queries) * scale
            return dot_nn(kt_s[col, there], score_grad)

        start = tuple(part(index, h, True) for h in range(heads))

        def step(tile, carry):
            return tuple(carry[h] + part(tile, h, False) for h in range(heads))

        done = lax.fori_loop(first_key_tile(index, splits), index, step, start)
        for h in range(heads):
            dq_s[here, cols[h]] += jnp.transpose(done[h]) * scale
        return 0

    lax.fori_loop(0, length // TILE, query_block, 0)
    for b in range(length // rows):
        dst = pl.ds(pl.multiple_of(order[b] * rows, rows), rows)
        src = slice(b * rows, (b + 1) * rows)
        proj_grad[dst, 0:width] = low(dq_s[src, :])
        proj_grad[dst, width : 2 * width] = low(dk_s[src, :])
        proj_grad[dst, 2 * width : 3 * width] = low(dv_s[src, :])


SMEM = pl.BlockSpec(memory_space=pltpu.SMEM)
VMEM = pl.BlockSpec(memory_space=pltpu.VMEM)


def attend_forward(order, splits, mix, proj, memory, norm, rows):
    heads, size, _ = memory.shape
    length, width = proj.shape[0], heads * size
    halves, tiles = length // SHORT, length // TILE
    shapes = [
        jax.ShapeDtypeStruct((length, width), jnp.bfloat16),
        jax.ShapeDtypeStruct((length, width), jnp.float32),
        jax.ShapeDtypeStruct((tiles, heads, TILE), jnp.float32),
        jax.ShapeDtypeStruct((halves, heads, size, size), jnp.float32),
        jax.ShapeDtypeStruct((halves, heads, size), jnp.float32),
        jax.ShapeDtypeStruct((heads, size, size), jnp.float32),
        jax.ShapeDtypeStruct((heads, size), jnp.float32),
    ]
    whole = pltpu.VMEM((length, width), jnp.bfloat16)
    return pl.pallas_call(
        functools.partial(forward_kernel, rows=rows, heads=heads, size=size),
        out_shape=shapes,
        in_specs=[SMEM] * 3 + [VMEM] * 3,
        out_specs=[VMEM] * len(shapes),
        scratch_shapes=[whole, whole, whole, pltpu.VMEM((width, length), jnp.bfloat16)],
        compiler_params=pltpu.CompilerParams(vmem_limit_bytes=VMEM_LIMIT),
        cost_estimate=NO_COST,
    )(order, splits, mix, proj, memory, norm)


def attend_backward(order, splits, mix, proj, combined_grad, attended, lse, states, norms, rows):
    _, heads, size, _ = states.shape
    length, width = proj.shape[0], heads * size
    tiles = length // TILE
    shapes = [
        jax.ShapeDtypeStruct((length, 3 * width), jnp.bfloat16),
        jax.ShapeDtypeStruct((heads, size), jnp.float32),
    ]
    whole = pltpu.VMEM((length, width), jnp.bfloat16)
    wide = pltpu.VMEM((length, width), jnp.float32)
    return pl.pallas_call(
        functools.partial(backward_kernel, rows=rows, heads=heads, size=size),
        out_shape=shapes,
        in_specs=[SMEM] * 3 + [VMEM] * 6,
        out_specs=[VMEM] * len(shapes),
        scratch_shapes=[
            whole, whole, whole, pltpu.VMEM((width, length), jnp.bfloat16), whole,
            pltpu.VMEM((tiles, heads, TILE), jnp.float32), wide, wide, wide,
        ],
        compiler_params=pltpu.CompilerParams(vmem_limit_bytes=VMEM_LIMIT),
        cost_estimate=NO_COST,
    )(order, splits, mix, proj, combined_grad, attended, lse, states, norms)


def fill(whole, pieces):
    rows = pieces[0].shape[0]
    for place, piece in enumerate(pieces):
        whole[place * rows : (place + 1) * rows, :] = piece[...]


def project_kernel(*refs, count):
    pieces, weight = refs[:count], refs[count]
    normed_all, proj_all = refs[-2:]
    width = normed_all.shape[1]

    @pl.when(pl.program_id(0) == 0)
    def _():
        begin = 0
        for piece in pieces:
            here = slice(begin, begin + piece.shape[0])
            normed_all[here, :] = piece[:, :width]
            begin += piece.shape[0]

    proj_all[...] = low(dot_nn(normed_all[...], weight[...]))


def widen_kernel(*refs, moves):
    out, parts = refs[-1], refs[:-1]
    for part, begin, size, place, column in moves:
        out[:, place, column : column + size] = parts[part][:, begin : begin + size].astype(jnp.float32)


def widen(parts, moves, shape):
    rows = shape[0]
    tall = min(rows, 128)
    return pl.pallas_call(
        functools.partial(widen_kernel, moves=moves),
        grid=(rows // tall,),
        out_shape=jax.ShapeDtypeStruct(shape, jnp.float32),
        in_specs=[pl.BlockSpec((tall, part.shape[1]), lambda i: (i, 0)) for part in parts],
        out_specs=pl.BlockSpec((tall, *shape[1:]), lambda i: (i, 0, 0)),
        cost_estimate=NO_COST,
    )(*parts)


def feed_kernel(*refs, count):
    normed, cots = refs[:count], refs[count : 2 * count]
    w_both, w_down = refs[2 * count : 2 * count + 2]
    result_s, grad_s = refs[-2:]
    results, grads = refs[-2 - 2 * count : -2 - count], refs[-2 - count : -2]
    normed_all, cot_all, hidden, first_grad, second_grad = refs[-7 - 2 * count : -2 - 2 * count]
    step = pl.program_id(0)
    half = pl.num_programs(0) // 2
    tile = w_down.shape[0]

    @pl.when(step == 0)
    def _():
        fill(normed_all, normed)
        fill(cot_all, cots)

    gate_up = dot_nn(normed_all[...], w_both[...])
    hidden_grad = dot_nt(cot_all[...], w_down[...])
    gate, up = gate_up[:, :tile], gate_up[:, tile:]
    sigmoid_gate = 1.0 / (1.0 + jnp.exp(-gate))
    activated = gate * sigmoid_gate
    low_hidden = low(activated * up)
    low_gate = low(hidden_grad * up * (sigmoid_gate + activated * (1.0 - sigmoid_gate)))
    low_up = low(hidden_grad * activated)
    hidden[...] = low_hidden
    both_grad = jnp.concatenate([low_gate, low_up], axis=1)

    @pl.when(step < half)
    def _():
        first_grad[...] = both_grad

    @pl.when(step >= half)
    def _():
        second_grad[...] = both_grad

    @pl.when(step == 0)
    def _():
        result_s[...] = dot_nn(low_hidden, w_down[...])
        grad_s[...] = dot_nt(both_grad, w_both[...])

    @pl.when(step > 0)
    def _():
        result_s[...] += dot_nn(low_hidden, w_down[...])
        grad_s[...] += dot_nt(both_grad, w_both[...])

    @pl.when(step == pl.num_programs(0) - 1)
    def _():
        rows = results[0].shape[0]
        for place in range(count):
            here = slice(place * rows, (place + 1) * rows)
            results[place][...] = low(result_s[here, :])
            grads[place][...] = low(grad_s[here, :])


NO_COST = pl.CostEstimate(flops=4_000_000_000, bytes_accessed=4096, transcendentals=0)
ANY = pl.BlockSpec(memory_space=pl.ANY)


def project_blocks(pieces, weight, place, length, before):
    width, wide = weight.shape
    count = len(pieces)
    tall = sum(piece.shape[0] for piece in pieces)
    tile = 256 if wide % 256 == 0 else 128
    return pl.pallas_call(
        functools.partial(project_kernel, count=count),
        grid=(wide // tile,),
        out_shape=[
            jax.ShapeDtypeStruct((length, width), jnp.bfloat16),
            jax.ShapeDtypeStruct((length, wide), jnp.bfloat16),
        ],
        in_specs=[pl.BlockSpec(piece.shape, lambda j: (0, 0)) for piece in pieces]
        + [pl.BlockSpec((width, tile), lambda j: (0, j))]
        + [ANY] * len(before),
        out_specs=[
            pl.BlockSpec((tall, width), lambda j: (place, 0)),
            pl.BlockSpec((tall, tile), lambda j: (place, j)),
        ],
        input_output_aliases={count + 1 + i: i for i in range(len(before))},
        compiler_params=pltpu.CompilerParams(vmem_limit_bytes=VMEM_LIMIT),
        cost_estimate=NO_COST,
    )(*pieces, weight, *before)


def feed_blocks(normed, cots, f_in, f_out, place, length, before):
    count = len(normed)
    rows, width = normed[0].shape
    tall, wide = count * rows, f_out.shape[0]
    tile = min(FEED_TILE, wide)
    tiles = wide // tile
    piece = pl.BlockSpec((rows, width), lambda j: (0, 0))
    kept = pl.BlockSpec((tall, width), lambda j: (place, 0))
    part = pl.BlockSpec((tall, tile), lambda j: (place, j))
    first = pl.BlockSpec((tall, 2 * tile), lambda j: (place, jnp.minimum(j, tiles // 2 - 1)))
    second = pl.BlockSpec((tall, 2 * tile), lambda j: (place, jnp.maximum(j - tiles // 2, 0)))
    outs = pl.pallas_call(
        functools.partial(feed_kernel, count=count),
        grid=(tiles,),
        out_shape=[jax.ShapeDtypeStruct((length, width), jnp.bfloat16)] * 2
        + [jax.ShapeDtypeStruct((length, wide), jnp.bfloat16)] * 3
        + [jax.ShapeDtypeStruct((rows, width), jnp.bfloat16)] * (2 * count),
        in_specs=[piece] * (2 * count)
        + [
            pl.BlockSpec((width, 2 * tile), lambda j: (0, j)),
            pl.BlockSpec((tile, width), lambda j: (j, 0)),
        ]
        + [ANY] * len(before),
        out_specs=[kept] * 2 + [part, first, second] + [piece] * (2 * count),
        scratch_shapes=[pltpu.VMEM((tall, width), jnp.float32)] * 2,
        input_output_aliases={2 * count + 2 + i: i for i in range(len(before))},
        compiler_params=pltpu.CompilerParams(vmem_limit_bytes=VMEM_LIMIT),
        cost_estimate=NO_COST,
    )(*normed, *cots, f_in, f_out, *before)
    return outs[:5], outs[5 : 5 + count], outs[5 + count :]


def ring_of(count):
    deep = 4 if count % 4 == 0 else count
    across = count // deep
    ring = [z * across for z in range(deep)]
    for z in reversed(range(deep)):
        turn = range(1, across)
        ring += [z * across + y for y in (turn if (deep - 1 - z) % 2 == 0 else reversed(turn))]
    return ring


class Ring:
    def __init__(self, count):
        self.count = count
        ring = ring_of(count)
        self.ahead = [(ring[p], ring[(p + 1) % count]) for p in range(count)]
        self.behind = [(b, a) for a, b in self.ahead]
        places = [0] * count
        for place, index in enumerate(ring):
            places[index] = place
        places = jnp.array(places, jnp.int32)
        self.slots = [0] * count
        self.slots[count // 2] = 1
        for step in range(1, count // 2):
            self.slots[count - step], self.slots[step] = 2 * step, 2 * step + 1
        here = places[lax.axis_index("blk")]
        self.order = jnp.array(self.slots, jnp.int32)[lax.rem(places - here + count, count)]
        around = lax.rem(jnp.arange(count, dtype=jnp.int32) + here, count)
        self.ahead_index = jnp.array(ring, jnp.int32)[around]

    def forth(self, values):
        return lax.ppermute(values, "blk", self.ahead)

    def back(self, values):
        return lax.ppermute(values, "blk", self.behind)


class Gather:
    def __init__(self, ring, block):
        self.ring = ring
        self.groups = [(block,)]

    def hop(self, *earlier):
        ring, half = self.ring, self.ring.count // 2
        last = self.groups[-1]
        behind, ahead = after((last[0], last[-1]), *earlier)
        if len(self.groups) == half:
            middle = behind.shape[0] // 2
            behind, ahead = behind[:middle], ahead[middle:]
        self.groups.append((ring.forth(behind), ring.back(ahead)))
        return self.groups[-1]

    def place(self, step):
        return {0: 0, self.ring.count // 2: 1}.get(step, step)


class Scatter:
    def __init__(self, ring, partial, axis=0):
        self.ring = ring
        self.partial = partial
        self.axis = axis
        self.step = ring.count // 2
        self.sent = self.moved = self.rider = self.parts = None
        self.begin = 0
        self.fresh = True

    def messages(self, *earlier):
        half, step = self.ring.count // 2, self.step
        self.step -= 1
        if step == half:
            return after(tuple(self.partial(half)), *earlier)
        forward, backward = self.came(*earlier)
        if step == half - 1:
            extra = forward.shape[self.axis]
            forward = jnp.pad(forward, [(0, extra if axis == self.axis else 0) for axis in (0, 1)])
            backward = jnp.pad(backward, [(extra if axis == self.axis else 0, 0) for axis in (0, 1)])
        parts = self.parts or (self.partial(step), self.partial(self.ring.count - step))
        self.parts = None
        forward, backward = parts[0].astype(jnp.float32) + forward, parts[1].astype(jnp.float32) + backward
        return low(forward), low(backward)

    def compute(self, *earlier):
        self.parts = after((low(self.partial(self.step)), low(self.partial(self.ring.count - self.step))), *earlier)

    def came(self, *earlier):
        width = self.partial(0).shape[1]
        return [
            part[:, self.begin : self.begin + width].astype(jnp.float32) for part in after(self.moved, *earlier)
        ]

    def prepare(self, *earlier, rider=None):
        self.sent = self.messages(*earlier)
        self.fresh = False
        self.rider = rider
        if rider is not None:
            self.sent = tuple(
                jnp.concatenate(pair, axis=1) for pair in zip(self.sent, rider.messages(*earlier))
            )
        self.sent = after(self.sent)

    def hop(self, *earlier):
        if self.fresh:
            self.prepare()
        self.fresh = True
        forward, backward = self.sent = after(self.sent, *earlier)
        self.moved = (self.ring.forth(forward), self.ring.back(backward))

    def hold(self, *others):
        self.moved = after(self.moved, *others)
        if self.rider is not None:
            self.rider.moved, self.rider.begin = self.moved, self.partial(0).shape[1]
            self.rider = None

    def total(self):
        forward, backward = self.came()
        return self.partial(0).astype(jnp.float32) + forward + backward


def after(values, *earlier):
    return lax.optimization_barrier((values, earlier))[0]


def sum_axis(values, axis):
    size = lax.axis_size(axis)
    terms = [values] + [
        lax.ppermute(values, axis, [(i, i ^ step) for i in range(size)]) for step in range(1, size)
    ]
    while len(terms) > 1:
        terms = [left + right for left, right in zip(terms[::2], terms[1::2])]
    return terms[0]


def swap_sum(values, axis, step, *earlier):
    size = lax.axis_size(axis)
    return values + after(lax.ppermute(values, axis, [(i, i ^ step) for i in range(size)]), *earlier)


def halve_rows(values, bit):
    size = lax.axis_size("seq")
    mine = lax.div(lax.axis_index("seq"), bit) % 2
    left = size // (2 * bit)
    blocks = values.reshape(left, 2, values.shape[0] // (2 * left), values.shape[1])
    kept = lax.dynamic_index_in_dim(blocks, mine, 1, keepdims=False)
    sent = lax.dynamic_index_in_dim(blocks, 1 - mine, 1, keepdims=False)
    moved = lax.ppermute(sent, "seq", [(i, i ^ bit) for i in range(size)])
    return low(kept.astype(jnp.float32) + moved.astype(jnp.float32)).reshape(-1, values.shape[1])


def rms_parts(values):
    scale_rows = lax.rsqrt(jnp.mean(values * values, axis=-1, keepdims=True) + EPSILON)
    return (scale_rows, values * scale_rows)


def rms_back(unit_grad, unit, scale_rows):
    return scale_rows * (unit_grad - unit * jnp.mean(unit_grad * unit, axis=-1, keepdims=True))


def sum_over_seq(values, dimension):
    return lax.psum_scatter(low(values), "seq", scatter_dimension=dimension, tiled=True)


def per_device(
    tokens,
    cotangent,
    grouping,
    memory_start,
    normalizer_start,
    gain_attention,
    attention_in,
    gate_logit,
    attention_out,
    gain_feed,
    feed_in,
    feed_out,
):
    rows, width = tokens.shape
    heads_here = memory_start.shape[1]
    count = lax.axis_size("blk")
    ring = Ring(count)
    splits = grouping[0]
    head_first = lax.axis_index("blk") * heads_here
    mix = jax.nn.sigmoid(lax.dynamic_slice_in_dim(gate_logit, head_first, heads_here, 0))

    def whole(weight, axis):
        return lax.all_gather(weight, "seq", axis=axis, tiled=True)

    half = count // 2
    tokens_full = tokens.astype(jnp.float32)
    scale_first, unit_first = rms_parts(tokens_full)

    length = rows * count
    w_in = whole(attention_in.reshape(attention_in.shape[0], -1), 0)
    gather_a = Gather(
        ring, jnp.concatenate([low(unit_first * gain_attention), attention_out.reshape(rows, -1)], axis=1)
    )

    gather_a.hop()
    feed_tile = min(FEED_TILE, feed_in.shape[2])
    feed_tiles = feed_in.shape[2] // feed_tile
    f_in = after(feed_in, gather_a.groups[0]).reshape(-1, 2, feed_tiles, feed_tile)
    f_in = f_in.transpose(0, 2, 1, 3).reshape(feed_in.shape[0], -1)
    f_in = whole(after(f_in, w_in, gather_a.groups[1]), 0)
    kept = []
    for step in range(2, half + 1):
        gather_a.hop()
        if step > 2:
            kept = project_blocks(gather_a.groups[step - 2], w_in, step - 2, length, kept)
    kept = project_blocks(gather_a.groups[half - 1], w_in, half - 1, length, kept)
    gather_a.groups[half] = after(gather_a.groups[half], kept[1])
    normed_a, proj = project_blocks(gather_a.groups[0] + gather_a.groups[half], w_in, 0, length, kept)
    w_out = jnp.zeros((length, gather_a.groups[0][0].shape[1] - width), jnp.bfloat16)
    for step, group in enumerate(gather_a.groups):
        for piece, d, begin in zip(group, (-step % count, step), (0, rows // 2 if step == half else 0)):
            start = ring.ahead_index[d] * rows + begin
            w_out = lax.dynamic_update_slice_in_dim(w_out, piece[:, width:], start, 0)
    w_out = whole(after(w_out.reshape(-1, attention_out.shape[1]), f_in), 1)

    gather_c = Gather(ring, after(cotangent, gather_a.groups[half]))
    gather_c.hop()
    merged, attended, lse, states, norms, memory_final, norm_final = attend_forward(
        ring.order, splits, mix, proj, memory_start[0], normalizer_start[0], rows
    )
    merged_mine = lax.all_to_all(after(merged, gather_c.groups[1]), "blk", 0, 1, tiled=True)
    f_out = whole(after(feed_out, w_out, merged_mine), 1)
    while len(gather_c.groups) < half - 1:
        gather_c.hop(merged_mine)
    middle = tokens_full + dot_nn(merged_mine, w_out)
    scale_second, unit_second = rms_parts(middle)
    gather_f = Gather(ring, after(low(unit_second * gain_feed), gather_c.groups[-1]))
    result_part, normed_f_part = {}, {}
    kept = []

    def feed(step, kept):
        kept, results, grads = feed_blocks(
            gather_f.groups[step], gather_c.groups[step], f_in, f_out, gather_f.place(step), length, kept
        )
        if step == half:
            result_part[half], normed_f_part[half] = results, grads
        else:
            for d, result, grad in zip((-step % count, step), results, grads):
                result_part[d], normed_f_part[d] = result, grad
        return kept

    for step in range(1, half + 1):
        gather_f.hop(gather_c.groups[-1], *kept[2:3])
        if step > 1:
            kept = feed(step - 1 if step < half else half, kept)
        if len(gather_c.groups) <= half:
            gather_c.hop(gather_f.groups[step], *(kept[2:3] if step > 1 else []))
        if step == 1:
            kept = feed(0, kept)
    kept = feed(half - 1, kept)
    normed_f, cot, hidden, first_grad, second_grad = kept

    scatter_f = Scatter(ring, lambda d: normed_f_part[d])
    scatter_r = Scatter(ring, lambda d: result_part[d])
    scatter_f.hop()
    scatter_r.hop(scatter_f.sent)
    scatter_f.hop(scatter_r.moved)
    for _ in range(half - 4):
        scatter_f.hop()
    feed_out_local = low(dot_tn(hidden, after(cot, scatter_f.sent)))
    scatter_f.hold(feed_out_local)
    feed_out_grad = sum_over_seq(after(feed_out_local, scatter_f.moved), 1)
    scatter_f.hop()
    feed_first_local = low(dot_tn(normed_f, after(first_grad, scatter_f.sent)))
    scatter_f.hold(feed_first_local)
    scatter_f.hop()
    feed_second_local = low(dot_tn(normed_f, after(second_grad, scatter_f.sent)))
    scatter_f.hold(feed_second_local)
    normed_f_grad = scatter_f.total()
    feed_first_grad = sum_over_seq(after(feed_first_local, feed_out_grad, normed_f_grad), 0)
    scatter_r.prepare()
    gain_feed_part = jnp.sum(normed_f_grad * unit_second, axis=0)
    middle_grad = cotangent.astype(jnp.float32) + rms_back(
        normed_f_grad * gain_feed, unit_second, scale_second
    )
    out_grad = low(middle_grad)
    combined_grad = low(dot_nt(out_grad, w_out))
    attention_out_local = low(dot_tn(merged_mine, after(out_grad, feed_second_local)))
    combined_grad = lax.all_to_all(combined_grad, "blk", 1, 0, tiled=True)
    combined_grad = after(combined_grad, attention_out_local, scatter_r.sent)
    out_sum = sum_over_seq(after(attention_out_local, feed_first_grad, combined_grad), 1)
    scatter_r.hop(combined_grad)
    proj_grad, gate_rows = attend_backward(
        ring.order, splits, mix, proj, combined_grad,
        attended, lse, states, norms, rows,
    )
    def in_two(values):
        return values[: values.shape[0] // 2], values[values.shape[0] // 2 :]

    def normed_a_part(d):
        first = ring.slots[d] * rows
        if d == half:
            return [low(dot_nt(part, w_in)) for part in in_two(proj_grad[first : first + rows])]
        return dot_nt(proj_grad[first : first + rows], w_in)

    proj_grad = after(proj_grad, scatter_r.moved)
    def attention_out_part(d):
        high = attention_out.shape[0]
        part = lax.dynamic_slice_in_dim(out_sum, ring.ahead_index[d] * high, high, 0).reshape(rows, -1)
        return (part[:, : part.shape[1] // 2], part[:, part.shape[1] // 2 :]) if d == half else part

    scatter_o = Scatter(ring, attention_out_part, axis=1)

    def rider():
        return scatter_o if scatter_o.step > 0 else None

    scatter_a = Scatter(ring, normed_a_part)
    scatter_a.hop()
    scatter_a.compute(scatter_a.sent)
    scatter_a.hold(scatter_a.parts)
    scatter_a.hop()
    scatter_r.prepare(scatter_a.sent, rider=rider())
    scatter_a.hold(scatter_r.sent)
    scatter_r.hop(scatter_a.moved)
    attention_in_local = low(dot_tn(normed_a, after(proj_grad, scatter_a.moved)))
    feed_second_grad = sum_over_seq(after(feed_second_local, out_sum, scatter_a.moved), 0)
    gain_attention_part = jnp.sum(attention_in_local.astype(jnp.float32) * w_in.astype(jnp.float32), axis=1) / gain_attention
    gate_part = jnp.sum(gate_rows, axis=1) * mix * (1.0 - mix)
    gate_full = lax.dynamic_update_slice_in_dim(
        jnp.zeros(gate_logit.shape, jnp.float32), gate_part, head_first, 0
    )
    sums = jnp.concatenate([gain_attention_part, gain_feed_part, gate_full])
    scatter_a.compute(scatter_a.moved)
    sums = sum_axis(sums, "seq")
    scatter_r.hold(scatter_a.parts, attention_in_local, sums)
    swaps = [1 << bit for bit in range(count.bit_length() - 1)]
    halvings = [1 << bit for bit in reversed(range(lax.axis_size("seq").bit_length() - 1))]
    attention_in_grad = attention_in_local
    while scatter_a.step > 1:
        scatter_a.prepare(rider=rider())
        scatter_a.hop(scatter_r.moved)
        if swaps:
            sums = swap_sum(after(sums, scatter_a.sent), "blk", swaps.pop())
        if halvings:
            attention_in_grad = halve_rows(after(attention_in_grad, scatter_a.sent), halvings.pop())
        scatter_a.hold(sums, attention_in_grad)
        scatter_r.prepare(rider=rider())
        scatter_r.hop(scatter_a.moved)
        scatter_a.compute(scatter_r.sent)
        if swaps:
            sums = swap_sum(after(sums, scatter_r.sent), "blk", swaps.pop())
        if halvings:
            attention_in_grad = halve_rows(after(attention_in_grad, scatter_r.sent), halvings.pop())
        scatter_r.hold(scatter_a.parts, sums, attention_in_grad)
    scatter_a.prepare(rider=rider())
    scatter_a.hop()
    sums = after(sums, scatter_a.sent)
    while len(swaps) > 1:
        sums = swap_sum(sums, "blk", swaps.pop())
    while halvings:
        attention_in_grad = halve_rows(after(attention_in_grad, scatter_a.sent), halvings.pop())
    halves = after((feed_first_grad, feed_second_grad), scatter_a.sent)
    moves = []
    for tile in range(feed_tiles):
        part, begin = divmod(2 * feed_tile * tile, feed_in.shape[2])
        for place in range(2):
            moves.append((part, begin + place * feed_tile, feed_tile, place, tile * feed_tile))
    feed_in_grad = widen(halves, moves, feed_in.shape)
    size = attention_in.shape[2]
    moves = [(0, place * size, size, place, 0) for place in range(attention_in.shape[1])]
    attention_in_grad = widen((after(attention_in_grad, scatter_a.sent),), moves, attention_in.shape)
    result, feed_out_grad = after((low(middle + scatter_r.total()), feed_out_grad), scatter_a.sent)
    feed_out_grad = feed_out_grad.astype(jnp.float32)
    while swaps:
        sums = swap_sum(sums, "blk", swaps.pop(), result, feed_in_grad, feed_out_grad, attention_in_grad)
    scatter_a.hold(sums)
    attention_out_grad = scatter_o.total().reshape(attention_out.shape)
    normed_a_grad = scatter_a.total()
    token_grad = middle_grad + rms_back(normed_a_grad * gain_attention, unit_first, scale_first)
    return (
        result,
        token_grad,
        sums[:width],
        attention_in_grad,
        sums[2 * width :],
        attention_out_grad.astype(jnp.float32),
        sums[width : 2 * width],
        feed_in_grad,
        feed_out_grad,
        memory_final[None],
        norm_final[None],
    )


def solution(mesh):
    in_specs = (
        P(("seq", "blk"), None),
        P(("seq", "blk"), None),
        P("seq", None),
        P("seq", "blk", None, None),
        P("seq", "blk", None),
        P(),
        P("seq", None, "blk"),
        P(),
        P("blk", "seq"),
        P(),
        P("seq", None, "blk"),
        P("blk", "seq"),
    )
    out_specs = (
        P(("seq", "blk"), None),
        P(("seq", "blk"), None),
        P(),
        P("seq", None, "blk"),
        P(),
        P("blk", "seq"),
        P(),
        P("seq", None, "blk"),
        P("blk", "seq"),
        P("seq", "blk", None, None),
        P("seq", "blk", None),
    )
    return jax.shard_map(
        per_device, mesh=mesh, in_specs=in_specs, out_specs=out_specs, check_vma=False
    )
```
